32 devices in a mesh: dp: 8 (over z, x), span: 2 (over y), tensor: 2 (over core).
Axes of the slice: x: 2, y: 2, z: 4, core: 2. Of those that a mesh axis runs over, the one named last changes fastest.
Arguments:
- queries: bfloat16 [8, 256, 4096], P('dp', 'span', 'tensor'), may hold values from -180 to 180
- key_states: bfloat16 [8, 256, 4096], P('dp', 'span', 'tensor'), may hold values from -6 to 6
- value_states: bfloat16 [8, 256, 4096], P('dp', 'span', 'tensor'), may hold values from -6 to 6
- out_grad: bfloat16 [8, 256, 4096], P('dp', None, 'span'), may hold values from -6 to 6
- out_weight: bfloat16 [4096, 4096], P('tensor', 'span'), may hold values from -0.09375 to 0.09375
- align_ids: int32 [8, 2, 2], P('dp', 'span'), may hold values from 0 to 1, as said below
- align_count: int32 [8, 2], P('dp', 'span'), may hold values from 1 to 2
Outputs:
- query_grad: bfloat16 [8, 256, 4096], P('dp', 'span', 'tensor')
- key_grad: bfloat16 [8, 256, 4096], P('dp', 'span', 'tensor')
- value_grad: bfloat16 [8, 256, 4096], P('dp', 'span', 'tensor')
- weight_grad: float32 [4096, 4096], P('tensor', 'span')
The draws below stay inside these ranges and needn't reach their ends.
Inputs may be any that keep to these rules, and one draw needn't show every extreme that they name: `align_ids`: each span's ids are distinct; block b is held by index b // 1 of span, span n by index n // 1, and every id of span n names a block whose holder differs from span n's holder by at most one.
All inputs are finite; a program needn't handle non-finite values.
Results may differ from the reference program's by a relative error of at most 0.033.
Values may be sent and summed in bfloat16 or wider, within the bound.
No kernel may reach another device: no remote copies, remote signals or barrier semaphores. Data moves between devices by JAX's collectives and lax.ppermute only.
A program may use at most 128 MiB of HBM per device.

```python
import math
import jax
import jax.numpy as jnp
from jax import lax

D = 4096
HEADS = 32
HEAD_DIM = 128
SPAN = 128
BLOCK = 128
ALIGN = 2
TGT_DEV = 128
SRC_DEV = 128
WIDTH = 4096
DOCS = 8
TGT = 256
SRC = 256
N_SPAN = 2


def keys_base(key):
    shape = (DOCS, SRC, HEADS * HEAD_DIM)
    base = jnp.clip(jax.random.normal(jax.random.fold_in(key, 11), shape, jnp.float32), -6.0, 6.0)
    return base


def align_base(key):
    span_total = TGT // SPAN
    block_total = SRC // BLOCK
    span_holder = jnp.arange(span_total) // (TGT_DEV // SPAN)
    block_holder = jnp.arange(block_total) // (SRC_DEV // BLOCK)
    near = jnp.abs(span_holder[:, None] - block_holder[None, :]) <= 1
    picks = jax.random.randint(jax.random.fold_in(key, 21), (DOCS, span_total, block_total), 0, 65536)
    ranked = jnp.where(near[None], picks * block_total + jnp.arange(block_total)[None, None, :], -1)
    best, _ = lax.top_k(ranked, ALIGN)
    return (best % block_total).astype(jnp.int32)


def draw_key_states(key, part):
    return keys_base(key).astype(jnp.bfloat16)


def draw_align_ids(key, part):
    return align_base(key)


def draw_queries(key, part):
    shape = (DOCS, TGT, HEADS * HEAD_DIM)
    base = jnp.clip(jax.random.normal(jax.random.fold_in(key, 31), shape, jnp.float32), -6.0, 6.0)
    return base.astype(jnp.bfloat16)


def touch_ends(drawn, key, low, top_value):
    shape = drawn.shape
    index_at = [jax.random.randint(jax.random.fold_in(key, axis), (), 0, shape[axis]) for axis in range(len(shape))]
    drawn = drawn.at[tuple(index_at)].set(low)
    longest = shape.index(max(shape))
    index_at[longest] = (index_at[longest] + 1) % shape[longest]
    return drawn.at[tuple(index_at)].set(top_value)


def shard_levels(own_key, dims, pieces, low, top_value):
    factor_of = 1.0
    for axis_at, blocks in pieces:
        draws = jax.random.uniform(jax.random.fold_in(jax.random.fold_in(own_key, 6), axis_at), (blocks,), jnp.float32, low / len(pieces), top_value / len(pieces))
        factor_of = factor_of * jnp.repeat(jnp.exp(draws), dims[axis_at] // blocks).reshape((-1,) + (1,) * (len(dims) - 1 - axis_at))
    return factor_of


def scatter_about(key, shape, scale, reach, split=(), kind=jnp.bfloat16):
    array = scale * jax.random.normal(key, shape, jnp.float32)
    if split:
        array = array * shard_levels(key, shape, split, -0.22, 0.18)
    return jnp.clip(array, -reach, reach).astype(kind)


def setup_inputs(seed: int = 0) -> dict:
    arg_keys = jax.random.split(jax.random.key(seed), 8)
    return {
        "queries": draw_queries(jax.random.fold_in(arg_keys[7], 71), 0),
        "key_states": draw_key_states(jax.random.fold_in(arg_keys[7], 71), 0),
        "value_states": scatter_about(arg_keys[2], (DOCS, SRC, WIDTH), 1.0, 6.0, ((0, 8), (1, 2), (2, 2))),
        "out_grad": scatter_about(arg_keys[3], (DOCS, TGT, D), 1.0, 6.0, ((0, 8), (2, 2))),
        "out_weight": scatter_about(arg_keys[4], (WIDTH, D), WIDTH ** -0.5, 0.09375, ((0, 2), (1, 2))),
        "align_ids": draw_align_ids(jax.random.fold_in(arg_keys[7], 71), 0),
        "align_count": touch_ends(jax.random.randint(arg_keys[6], (DOCS, TGT // SPAN), 1, ALIGN + 1), jax.random.fold_in(arg_keys[6], 1), 1, ALIGN).astype(jnp.int32),
    }


def reference(queries, key_states, value_states, out_grad, out_weight, align_ids, align_count):
    f32 = jnp.float32
    b16 = jnp.bfloat16
    scale = 1.0 / math.sqrt(HEAD_DIM)
    width = HEADS * HEAD_DIM
    column_group = D // N_SPAN
    spans_doc = TGT // SPAN
    blocks_doc = SRC // BLOCK
    spans_device = TGT_DEV // SPAN
    blocks_device = SRC_DEV // BLOCK

    def one_doc(grad_total, inputs):
        query, key_doc, value_doc, grad_doc, idents, counts = inputs
        context_grad = jnp.zeros((TGT, width), f32)
        for group in range(N_SPAN):
            left = group * column_group
            partial_term = jnp.dot(grad_doc[:, left:left + column_group], out_weight[:, left:left + column_group].T, preferred_element_type=f32)
            context_grad = context_grad + partial_term.astype(b16).astype(f32)
        context_grad = context_grad.astype(b16)
        query_heads = query.reshape(spans_doc, SPAN, HEADS, HEAD_DIM).astype(f32)
        key_near = key_doc.reshape(blocks_doc, BLOCK, width)[idents].reshape(spans_doc, ALIGN * BLOCK, HEADS, HEAD_DIM).astype(f32)
        value_near = value_doc.reshape(blocks_doc, BLOCK, width)[idents].reshape(spans_doc, ALIGN * BLOCK, HEADS, HEAD_DIM).astype(f32)
        live = (jnp.arange(ALIGN * BLOCK) // BLOCK)[None, :] < counts[:, None]
        mask = live[:, None, None, :]
        scores = jnp.einsum('nqhd,nkhd->nhqk', query_heads, key_near) * scale
        masked = jnp.where(mask, scores, -1e+30)
        top = lax.optimization_barrier(jnp.max(masked, axis=-1, keepdims=True))
        weights = jnp.where(mask, jnp.exp(masked - top), 0.0)
        prob = weights / lax.optimization_barrier(jnp.sum(weights, axis=-1, keepdims=True))
        prob_half = prob.astype(b16).astype(f32)
        context = jnp.einsum('nhqk,nkhd->nqhd', prob_half, value_near).astype(b16)
        grad_heads = context_grad.reshape(spans_doc, SPAN, HEADS, HEAD_DIM).astype(f32)
        dprob = jnp.einsum('nqhd,nkhd->nhqk', grad_heads, value_near)
        delta = jnp.einsum('nqhd,nqhd->nhq', grad_heads, context.astype(f32))[..., None]
        dscore = (prob * (dprob - delta)).astype(b16).astype(f32)
        query_grad = (jnp.einsum('nhqk,nkhd->nqhd', dscore, key_near) * scale).astype(b16)
        key_term = jnp.einsum('nhqk,nqhd->nkhd', dscore, query_heads) * scale
        value_term = jnp.einsum('nhqk,nqhd->nkhd', prob_half, grad_heads)
        stacked = jnp.stack([key_term, value_term]).reshape(2, spans_doc, ALIGN, BLOCK, width)
        onehot = (idents[:, :, None] == jnp.arange(blocks_doc)[None, None, :]).astype(f32)
        span_holder = jnp.arange(spans_doc) // spans_device
        block_holder = jnp.arange(blocks_doc) // blocks_device
        total = jnp.zeros((2, blocks_doc, BLOCK, width), f32)
        for group in range(N_SPAN):
            select = (span_holder == group).astype(f32)[:, None, None] * onehot
            part_sum = jnp.einsum('nab,knaxw->kbxw', select, stacked, precision=lax.Precision.HIGHEST)
            rounded = lax.optimization_barrier(part_sum.astype(b16)).astype(f32)
            keep = (block_holder == group)[None, :, None, None]
            total = total + jnp.where(keep, part_sum, rounded)
        key_grad = total[0].reshape(SRC, width).astype(b16)
        value_grad = total[1].reshape(SRC, width).astype(b16)
        grad_total = grad_total + jnp.dot(context.reshape(TGT, width).T, grad_doc, preferred_element_type=f32)
        return (grad_total, (query_grad.reshape(TGT, width), key_grad, value_grad))
    start_total = jnp.zeros((width, D), f32)
    weight_grad, outs = lax.scan(one_doc, start_total, (queries, key_states, value_states, out_grad, align_ids.astype(jnp.int32), align_count.astype(jnp.int32)))
    return (outs[0], outs[1], outs[2], weight_grad)
```

```python
import math

import jax
import jax.numpy as jnp
from jax import lax
from jax.sharding import PartitionSpec as P

HEAD_DIM = 128
SPAN = 128
BLOCK = 128
ALIGN = 2


def with_halo(block, sides, width):
    for axis, dim in sides:
        count = lax.axis_size(axis)
        forward = [(i, i + 1) for i in range(count - 1)]
        backward = [(target, source) for source, target in forward]
        low = lax.ppermute(
            lax.slice_in_dim(block, block.shape[dim] - width, None, axis=dim), axis, forward
        )
        high = lax.ppermute(lax.slice_in_dim(block, 0, width, axis=dim), axis, backward)
        block = jnp.concatenate([low, block, high], axis=dim)
    return block


def shifted(value, axis, steps):
    count = lax.axis_size(axis)
    initial, last = (max(0, -steps), min(count, count - steps))
    return lax.ppermute(value, axis, [(source, source + steps) for source in range(initial, last)])


def shards(queries, key_states, value_states, out_grad, out_weight, align_ids, align_count):
    f32 = jnp.float32
    b16 = jnp.bfloat16
    scale = 1.0 / math.sqrt(HEAD_DIM)
    local_width = queries.shape[2]
    local_heads = local_width // HEAD_DIM
    target_rows = queries.shape[1]
    source_rows = key_states.shape[1]
    span_number = target_rows // SPAN
    block_number = source_rows // BLOCK
    grad_rows = out_grad[0]
    context_grad = (
        lax.psum_scatter(
            lax.dot_general(
                grad_rows, out_weight, (((1,), (1,)), ((), ())), preferred_element_type=f32
            ).astype(jnp.bfloat16),
            "span",
            scatter_dimension=0,
            tiled=True,
        )
        .astype(jnp.float32)
        .astype(b16)
    )
    stacked = jnp.stack([key_states[0], value_states[0]])
    panel = with_halo(stacked, (("span", 1),), source_rows)
    position = lax.axis_index("span")
    local_ids = align_ids[0] - (position - 1) * block_number
    panel_blocks = panel.reshape(2, 3 * block_number, BLOCK, local_width)
    fetched = panel_blocks[:, local_ids]
    key_near = fetched[0].reshape(span_number, ALIGN * BLOCK, local_heads, HEAD_DIM)
    value_near = fetched[1].reshape(span_number, ALIGN * BLOCK, local_heads, HEAD_DIM)
    query_heads = queries[0].reshape(span_number, SPAN, local_heads, HEAD_DIM)
    live = (jnp.arange(ALIGN * BLOCK) // BLOCK)[None, :] < align_count[0][:, None]
    mask = live[:, None, None, :]
    scores = (
        jnp.einsum("nqhd,nkhd->nhqk", query_heads, key_near, preferred_element_type=f32) * scale
    )
    masked = jnp.where(mask, scores, -1e30)
    top = jnp.max(masked, axis=-1, keepdims=True)
    weights = jnp.where(mask, jnp.exp(masked - top), 0.0)
    prob = weights / jnp.sum(weights, axis=-1, keepdims=True)
    prob_half = prob.astype(b16)
    context = jnp.einsum(
        "nhqk,nkhd->nqhd", prob_half, value_near, preferred_element_type=f32
    ).astype(b16)
    grad_heads = context_grad.reshape(span_number, SPAN, local_heads, HEAD_DIM)
    dprob = jnp.einsum("nqhd,nkhd->nhqk", grad_heads, value_near, preferred_element_type=f32)
    delta = jnp.einsum("nqhd,nqhd->nhq", grad_heads, context, preferred_element_type=f32)[..., None]
    dscore = (prob * (dprob - delta)).astype(b16)
    query_grad = (
        jnp.einsum("nhqk,nkhd->nqhd", dscore, key_near, preferred_element_type=f32) * scale
    ).astype(b16)
    key_term = (
        jnp.einsum("nhqk,nqhd->nkhd", dscore, query_heads, preferred_element_type=f32) * scale
    )
    value_term = jnp.einsum("nhqk,nqhd->nkhd", prob_half, grad_heads, preferred_element_type=f32)
    slot_terms = jnp.stack([key_term, value_term]).reshape(
        2, span_number * ALIGN, BLOCK, local_width
    )
    flat_ids = local_ids.reshape(span_number * ALIGN)
    spread = (
        jnp.zeros((2, 3 * block_number, BLOCK, local_width), f32).at[:, flat_ids].add(slot_terms)
    )
    spread = spread.reshape(2, 3 * source_rows, local_width)
    lower_rim = spread[:, :source_rows].astype(b16)
    upper_rim = spread[:, 2 * source_rows :].astype(b16)
    from_above = shifted(lower_rim, "span", -1)
    from_below = shifted(upper_rim, "span", 1)
    summed = (
        spread[:, source_rows : 2 * source_rows] + from_above.astype(f32) + from_below.astype(f32)
    )
    pair_grad = summed.astype(b16)
    flat_context = context.reshape(target_rows, local_width)
    documents = lax.axis_size("dp")
    tokens = documents * grad_rows.shape[0]
    columns = grad_rows.shape[1]
    if tokens * (local_width + columns) <= 2 * local_width * columns:
        cores = lax.axis_size("tensor")
        share = grad_rows.shape[0] // cores
        own_share = lax.dynamic_slice_in_dim(
            grad_rows, lax.axis_index("tensor") * share, share, axis=0
        )
        all_grad = lax.all_gather(own_share, ("dp", "tensor"), axis=0, tiled=True)
        all_context = lax.all_gather(flat_context, ("dp", "span"), axis=0, tiled=True)
        weight_grad = lax.dot_general(
            all_context, all_grad, (((0,), (0,)), ((), ())), preferred_element_type=f32
        )
    else:
        gathered = lax.all_gather(flat_context, "span", axis=0, tiled=True)
        partial_grad = lax.dot_general(
            gathered, grad_rows, (((0,), (0,)), ((), ())), preferred_element_type=f32
        )
        weight_grad = lax.psum(partial_grad, "dp")
    query_out = query_grad.reshape(1, target_rows, local_width)
    return (query_out, pair_grad[0][None], pair_grad[1][None], weight_grad)


def solution(mesh):
    return jax.shard_map(
        shards,
        mesh=mesh,
        in_specs=(
            P("dp", "span", "tensor"),
            P("dp", "span", "tensor"),
            P("dp", "span", "tensor"),
            P("dp", None, "span"),
            P("tensor", "span"),
            P("dp", "span", None),
            P("dp", "span"),
        ),
        out_specs=(
            P("dp", "span", "tensor"),
            P("dp", "span", "tensor"),
            P("dp", "span", "tensor"),
            P("tensor", "span"),
        ),
        check_vma=False,
    )
```

```python
import math

import jax
import jax.numpy as jnp
from jax import lax
from jax.experimental import pallas as pl
from jax.experimental.pallas import tpu as pltpu
from jax.sharding import PartitionSpec as P

HEAD_DIM = 128
SPAN = 128
BLOCK = 128
ALIGN = 2


def with_halo(block, sides, width):
    for axis, dim in sides:
        count = lax.axis_size(axis)
        forward = [(i, i + 1) for i in range(count - 1)]
        backward = [(target, source) for source, target in forward]
        low = lax.ppermute(
            lax.slice_in_dim(block, block.shape[dim] - width, None, axis=dim), axis, forward
        )
        high = lax.ppermute(lax.slice_in_dim(block, 0, width, axis=dim), axis, backward)
        block = jnp.concatenate([low, block, high], axis=dim)
    return block


def shifted(value, axis, steps):
    count = lax.axis_size(axis)
    initial, last = (max(0, -steps), min(count, count - steps))
    return lax.ppermute(value, axis, [(source, source + steps) for source in range(initial, last)])


NT = (((1,), (1,)), ((), ()))
TN = (((0,), (0,)), ((), ()))
NN = (((1,), (0,)), ((), ()))


def dot(a, b, dims):
    return lax.dot_general(a, b, dims, preferred_element_type=jnp.float32)


def ordered(first, own, peer):
    return jnp.where(
        first, jnp.concatenate([own, peer], axis=0), jnp.concatenate([peer, own], axis=0)
    )


def forward_kernel(scale, info, q_own, k_own, v_own, q_peer, k_peer, v_peer, prob_ref, context_ref):
    first = info[0] == 0
    q = ordered(first, q_own[...], q_peer[0])
    k = ordered(first, k_own[...], k_peer[0])
    v = ordered(first, v_own[...], v_peer[0])
    scores = dot(k, q, NT) * scale
    lane = lax.broadcasted_iota(jnp.int32, (1, 2 * SPAN), 1) < SPAN
    bias = [
        jnp.where(jnp.where(lane, info[1 + b], info[3 + b]) > 0, 0.0, -1e30) for b in range(2)
    ]
    scores = jnp.concatenate([scores[:BLOCK] + bias[0], scores[BLOCK:] + bias[1]], axis=0)
    weights = jnp.exp(scores - jnp.max(scores, axis=0, keepdims=True))
    prob = weights * (1.0 / jnp.sum(weights, axis=0, keepdims=True))
    prob_ref[0] = prob
    context_ref[...] = dot(v, prob.astype(jnp.bfloat16), TN).astype(jnp.bfloat16)


def backward_kernel(
    scale, info, q_own, k_own, v_own, q_peer, k_peer, v_peer, prob_ref, cg_own, cg_peer, kept, sent
):
    b16 = jnp.bfloat16
    first = info[0] == 0
    q = ordered(first, q_own[...], q_peer[0])
    k = ordered(first, k_own[...], k_peer[0])
    v = ordered(first, v_own[...], v_peer[0])
    cg = (cg_own[...].astype(jnp.float32) + cg_peer[...].astype(jnp.float32)).astype(b16)
    prob = prob_ref[0]
    dprob = dot(v, cg, NT)
    delta = jnp.sum(prob * dprob, axis=0, keepdims=True)
    dscore = (prob * (dprob - delta)).astype(b16)
    grads = (
        (dot(dscore, k, TN) * scale).astype(b16),
        (dot(dscore, q, NN) * scale).astype(b16),
        dot(prob.astype(b16), cg, NN).astype(b16),
    )
    for i, grad in enumerate(grads):
        kept[i] = jnp.where(first, grad[:SPAN], grad[SPAN:])
        sent[i] = jnp.where(first, grad[SPAN:], grad[:SPAN])


def weight_kernel(count, *refs):
    left, right, out = refs[1 : 1 + count], refs[1 + count : 1 + 2 * count], refs[-1]
    rows = out.shape[0]
    step = min(256, rows)
    for r in range(0, rows, step):
        total = dot(left[0][r : r + step], right[0][...], NN)
        for a, b in zip(left[1:], right[1:]):
            total += dot(a[r : r + step], b[...], NN)
        out[r : r + step] = total


def weight_block(place, left, right, held, width):
    count = len(left)
    rows, depth = left[0].shape
    columns = right[0].shape[1]
    tile = 256
    tiles = columns // tile
    in_specs = [pl.BlockSpec((rows, depth), lambda j, p: (0, 0))] * count
    in_specs += [pl.BlockSpec((depth, tile), lambda j, p: (0, j))] * count
    operands = [place, *left, *right]
    aliases = {}
    if held is not None:
        in_specs.append(pl.BlockSpec(memory_space=pl.ANY))
        operands.append(held)
        aliases = {len(operands) - 1: 0}
    return pl.pallas_call(
        lambda *refs: weight_kernel(count, *refs),
        grid_spec=pltpu.PrefetchScalarGridSpec(
            num_scalar_prefetch=1,
            grid=(tiles,),
            in_specs=in_specs,
            out_specs=pl.BlockSpec((rows, tile), lambda j, p: (p[0], p[1] * tiles + j)),
        ),
        out_shape=jax.ShapeDtypeStruct((width[0], width[1]), jnp.float32),
        input_output_aliases=aliases,
        compiler_params=pltpu.CompilerParams(vmem_limit_bytes=40 * 2**20),
        cost_estimate=pl.CostEstimate(
            flops=2 * rows * depth * count * columns,
            bytes_accessed=4 * rows * columns + 2 * count * depth * (rows + columns),
            transcendentals=0,
        ),
    )(*operands)


def exchange(value, axis, bits):
    count = lax.axis_size(axis)
    return lax.ppermute(value, axis, [(i, i ^ bits) for i in range(count)])


def paired(queries, key_states, value_states, out_grad, out_weight, align_ids, align_count):
    f32 = jnp.float32
    b16 = jnp.bfloat16
    scale = 1.0 / math.sqrt(HEAD_DIM)
    width = queries.shape[2]
    half = width // 2
    heads = half // HEAD_DIM
    rows = queries.shape[1]
    tokens, columns = out_grad.shape[1:]
    core_columns = columns // 2
    y = lax.axis_index("span")
    t = lax.axis_index("tensor")

    def part(value, which):
        return lax.dynamic_slice_in_dim(value, which * half, half, axis=1)

    own = (queries[0], key_states[0], value_states[0])
    peer = exchange(jnp.stack([part(v, 1 - y) for v in own]), "span", 1)
    slot = jnp.arange(ALIGN)
    live = jnp.stack(
        [jnp.any((align_ids[0, 0] == b) & (slot < align_count[0, 0])) for b in range(2)]
    ).astype(jnp.int32)
    live_peer = exchange(jnp.broadcast_to(live[:, None], (2, 128)), "span", 1)[:, 0]
    live = jnp.where(y == 0, jnp.concatenate([live, live_peer]), jnp.concatenate([live_peer, live]))
    info = jnp.concatenate([jnp.reshape(y, (1,)).astype(jnp.int32), live])

    grad_rows = out_grad[0]
    grads = [lax.dynamic_slice_in_dim(grad_rows, t * core_columns, core_columns, axis=1)]
    grads += [exchange(grads[0], "dp", 2 * k) for k in range(1, 4)]
    grads += [exchange(g, "dp", 1) for g in grads]
    grads_core = [lax.dynamic_slice_in_dim(grad_rows, (1 - t) * core_columns, core_columns, axis=1)]
    grads_core += [exchange(g, "tensor", 1) for g in grads[1:]]

    partial = dot(grad_rows, out_weight, NT).astype(b16)
    partial_peer = exchange(part(partial, 1 - y), "span", 1)

    own_spec = pl.BlockSpec((rows, HEAD_DIM), lambda h, info: (0, info[0] * heads + h))
    peer_specs = [
        pl.BlockSpec((1, rows, HEAD_DIM), lambda h, info, i=i: (i, 0, h)) for i in range(3)
    ]
    prob_spec = pl.BlockSpec((1, 2 * BLOCK, 2 * SPAN), lambda h, info: (h, 0, 0))
    prob, context = pl.pallas_call(
        lambda *refs: forward_kernel(scale, *refs),
        grid_spec=pltpu.PrefetchScalarGridSpec(
            num_scalar_prefetch=1,
            grid=(heads,),
            in_specs=[own_spec] * 3 + peer_specs,
            out_specs=[prob_spec, pl.BlockSpec((HEAD_DIM, 2 * SPAN), lambda h, info: (h, 0))],
        ),
        out_shape=[
            jax.ShapeDtypeStruct((heads, 2 * BLOCK, 2 * SPAN), f32),
            jax.ShapeDtypeStruct((half, 2 * SPAN), b16),
        ],
        cost_estimate=pl.CostEstimate(
            flops=heads * 2**25, bytes_accessed=5 * 2**20, transcendentals=heads * 2**16
        ),
    )(info, *own, peer, peer, peer)

    near = [context] + [exchange(context, "dp", 2 * k) for k in range(1, 4)]
    near_x = [exchange(c, "dp", 1) for c in near]
    far = [exchange(c, "span", 1) for c in near]
    far_x = [exchange(c, "span", 1) for c in near_x[:2]] + [exchange(c, "dp", 1) for c in far[2:]]

    cg_own = pl.BlockSpec((tokens, HEAD_DIM), lambda h, info: (0, info[0] * heads + h))
    cg_peer = pl.BlockSpec((tokens, HEAD_DIM), lambda h, info: (0, h))
    out_spec = pl.BlockSpec((3, rows, HEAD_DIM), lambda h, info: (0, 0, h))
    kept, sent = pl.pallas_call(
        lambda *refs: backward_kernel(scale, *refs),
        grid_spec=pltpu.PrefetchScalarGridSpec(
            num_scalar_prefetch=1,
            grid=(heads,),
            in_specs=[own_spec] * 3 + peer_specs + [prob_spec, cg_own, cg_peer],
            out_specs=[out_spec, out_spec],
        ),
        out_shape=[jax.ShapeDtypeStruct((3, rows, half), b16)] * 2,
        cost_estimate=pl.CostEstimate(
            flops=heads * 2**26, bytes_accessed=6 * 2**20, transcendentals=0
        ),
    )(info, *own, peer, peer, peer, prob, partial, partial_peer)
    received = exchange(sent, "span", 1)
    outs = [
        jnp.where(
            y == 0,
            jnp.concatenate([kept[i], received[i]], axis=1),
            jnp.concatenate([received[i], kept[i]], axis=1),
        )[None]
        for i in range(3)
    ]

    weight_grad = None
    shape = (width, columns)
    for row, left in ((y, near + near_x), (1 - y, far + far_x)):
        for column, right in ((t, grads), (1 - t, grads_core)):
            place = jnp.stack([row, column]).astype(jnp.int32)
            weight_grad = weight_block(place, left, right, weight_grad, shape)
    return (*outs, weight_grad)


def shards(queries, key_states, value_states, out_grad, out_weight, align_ids, align_count):
    two_spans = lax.axis_size("span") == 2 and queries.shape[1] == SPAN == key_states.shape[1]
    if two_spans and lax.axis_size("dp") == 8 and lax.axis_size("tensor") == 2:
        return paired(
            queries, key_states, value_states, out_grad, out_weight, align_ids, align_count
        )
    f32 = jnp.float32
    b16 = jnp.bfloat16
    scale = 1.0 / math.sqrt(HEAD_DIM)
    local_width = queries.shape[2]
    local_heads = local_width // HEAD_DIM
    target_rows = queries.shape[1]
    source_rows = key_states.shape[1]
    span_number = target_rows // SPAN
    block_number = source_rows // BLOCK
    grad_rows = out_grad[0]
    context_grad = (
        lax.psum_scatter(
            lax.dot_general(
                grad_rows, out_weight, (((1,), (1,)), ((), ())), preferred_element_type=f32
            ).astype(jnp.bfloat16),
            "span",
            scatter_dimension=0,
            tiled=True,
        )
        .astype(jnp.float32)
        .astype(b16)
    )
    stacked = jnp.stack([key_states[0], value_states[0]])
    panel = with_halo(stacked, (("span", 1),), source_rows)
    position = lax.axis_index("span")
    local_ids = align_ids[0] - (position - 1) * block_number
    panel_blocks = panel.reshape(2, 3 * block_number, BLOCK, local_width)
    fetched = panel_blocks[:, local_ids]
    key_near = fetched[0].reshape(span_number, ALIGN * BLOCK, local_heads, HEAD_DIM)
    value_near = fetched[1].reshape(span_number, ALIGN * BLOCK, local_heads, HEAD_DIM)
    query_heads = queries[0].reshape(span_number, SPAN, local_heads, HEAD_DIM)
    live = (jnp.arange(ALIGN * BLOCK) // BLOCK)[None, :] < align_count[0][:, None]
    mask = live[:, None, None, :]
    scores = (
        jnp.einsum("nqhd,nkhd->nhqk", query_heads, key_near, preferred_element_type=f32) * scale
    )
    masked = jnp.where(mask, scores, -1e30)
    top = jnp.max(masked, axis=-1, keepdims=True)
    weights = jnp.where(mask, jnp.exp(masked - top), 0.0)
    prob = weights / jnp.sum(weights, axis=-1, keepdims=True)
    prob_half = prob.astype(b16)
    context = jnp.einsum(
        "nhqk,nkhd->nqhd", prob_half, value_near, preferred_element_type=f32
    ).astype(b16)
    grad_heads = context_grad.reshape(span_number, SPAN, local_heads, HEAD_DIM)
    dprob = jnp.einsum("nqhd,nkhd->nhqk", grad_heads, value_near, preferred_element_type=f32)
    delta = jnp.einsum("nqhd,nqhd->nhq", grad_heads, context, preferred_element_type=f32)[..., None]
    dscore = (prob * (dprob - delta)).astype(b16)
    query_grad = (
        jnp.einsum("nhqk,nkhd->nqhd", dscore, key_near, preferred_element_type=f32) * scale
    ).astype(b16)
    key_term = (
        jnp.einsum("nhqk,nqhd->nkhd", dscore, query_heads, preferred_element_type=f32) * scale
    )
    value_term = jnp.einsum("nhqk,nqhd->nkhd", prob_half, grad_heads, preferred_element_type=f32)
    slot_terms = jnp.stack([key_term, value_term]).reshape(
        2, span_number * ALIGN, BLOCK, local_width
    )
    flat_ids = local_ids.reshape(span_number * ALIGN)
    spread = (
        jnp.zeros((2, 3 * block_number, BLOCK, local_width), f32).at[:, flat_ids].add(slot_terms)
    )
    spread = spread.reshape(2, 3 * source_rows, local_width)
    lower_rim = spread[:, :source_rows].astype(b16)
    upper_rim = spread[:, 2 * source_rows :].astype(b16)
    from_above = shifted(lower_rim, "span", -1)
    from_below = shifted(upper_rim, "span", 1)
    summed = (
        spread[:, source_rows : 2 * source_rows] + from_above.astype(f32) + from_below.astype(f32)
    )
    pair_grad = summed.astype(b16)
    flat_context = context.reshape(target_rows, local_width)
    documents = lax.axis_size("dp")
    tokens = documents * grad_rows.shape[0]
    columns = grad_rows.shape[1]
    if tokens * (local_width + columns) <= 2 * local_width * columns:
        cores = lax.axis_size("tensor")
        share = grad_rows.shape[0] // cores
        own_share = lax.dynamic_slice_in_dim(
            grad_rows, lax.axis_index("tensor") * share, share, axis=0
        )
        all_grad = lax.all_gather(own_share, ("dp", "tensor"), axis=0, tiled=True)
        all_context = lax.all_gather(flat_context, ("dp", "span"), axis=0, tiled=True)
        weight_grad = lax.dot_general(
            all_context, all_grad, (((0,), (0,)), ((), ())), preferred_element_type=f32
        )
    else:
        gathered = lax.all_gather(flat_context, "span", axis=0, tiled=True)
        partial_grad = lax.dot_general(
            gathered, grad_rows, (((0,), (0,)), ((), ())), preferred_element_type=f32
        )
        weight_grad = lax.psum(partial_grad, "dp")
    query_out = query_grad.reshape(1, target_rows, local_width)
    return (query_out, pair_grad[0][None], pair_grad[1][None], weight_grad)


def solution(mesh):
    return jax.shard_map(
        shards,
        mesh=mesh,
        in_specs=(
            P("dp", "span", "tensor"),
            P("dp", "span", "tensor"),
            P("dp", "span", "tensor"),
            P("dp", None, "span"),
            P("tensor", "span"),
            P("dp", "span", None),
            P("dp", "span"),
        ),
        out_specs=(
            P("dp", "span", "tensor"),
            P("dp", "span", "tensor"),
            P("dp", "span", "tensor"),
            P("tensor", "span"),
        ),
        check_vma=False,
    )
```

```python
import math

import jax
import jax.numpy as jnp
from jax import lax
from jax.experimental import pallas as pl
from jax.experimental.pallas import tpu as pltpu
from jax.sharding import PartitionSpec as P

HEAD_DIM = 128
SPAN = 128
BLOCK = 128
ALIGN = 2


def with_halo(block, sides, width):
    for axis, dim in sides:
        count = lax.axis_size(axis)
        forward = [(i, i + 1) for i in range(count - 1)]
        backward = [(target, source) for source, target in forward]
        low = lax.ppermute(
            lax.slice_in_dim(block, block.shape[dim] - width, None, axis=dim), axis, forward
        )
        high = lax.ppermute(lax.slice_in_dim(block, 0, width, axis=dim), axis, backward)
        block = jnp.concatenate([low, block, high], axis=dim)
    return block


def shifted(value, axis, steps):
    count = lax.axis_size(axis)
    initial, last = (max(0, -steps), min(count, count - steps))
    return lax.ppermute(value, axis, [(source, source + steps) for source in range(initial, last)])


NT = (((1,), (1,)), ((), ()))
TN = (((0,), (0,)), ((), ()))
NN = (((1,), (0,)), ((), ()))
MIB = 2**20
FLAG_ROWS = 16


def dot(a, b, dims):
    return lax.dot_general(a, b, dims, preferred_element_type=jnp.float32)


def ordered(first, own, peer, axis):
    return jnp.where(
        first, jnp.concatenate([own, peer], axis=axis), jnp.concatenate([peer, own], axis=axis)
    )


def call(kernel, place, grid, inputs, outputs, cost, aliases=None, scratch=(), vmem=60):
    flops, moved, exps = cost
    return pl.pallas_call(
        kernel,
        grid_spec=pltpu.PrefetchScalarGridSpec(
            num_scalar_prefetch=1,
            grid=grid,
            in_specs=[spec for _, spec in inputs],
            out_specs=[spec for _, _, spec in outputs],
            scratch_shapes=list(scratch),
        ),
        out_shape=[jax.ShapeDtypeStruct(shape, dtype) for shape, dtype, _ in outputs],
        input_output_aliases=aliases or {},
        compiler_params=pltpu.CompilerParams(vmem_limit_bytes=vmem * MIB),
        cost_estimate=pl.CostEstimate(flops=flops, bytes_accessed=moved, transcendentals=exps),
    )(place, *[array for array, _ in inputs])


def live_flags(ids, count, shape):
    row = lax.broadcasted_iota(jnp.int32, shape, 0)
    found = jnp.zeros(shape, jnp.float32)
    for slot in range(ALIGN):
        alive = slot < count[0, 0]
        found += jnp.where((row == ids[0, 0, slot]) & alive, 1.0, 0.0)
    return found


def prepare_kernel(place, q, k, v, ids, count, packed):
    rows = q.shape[1]
    for i, ref in enumerate((q, k, v)):
        packed[i * rows : (i + 1) * rows] = ref[0]
    packed[3 * rows :] = live_flags(ids, count, (FLAG_ROWS, q.shape[2])).astype(jnp.bfloat16)


def head_of(first, own, packed, h):
    at = slice(h * HEAD_DIM, (h + 1) * HEAD_DIM)
    rows = own[0].shape[1]
    return at, [
        ordered(first, ref[0, :, at], packed[i * rows : (i + 1) * rows, at], 0)
        for i, ref in enumerate(own)
    ]


def block_bias(first, packed, ids, count):
    flags = packed.shape[0] - FLAG_ROWS
    live = live_flags(ids, count, (FLAG_ROWS, SPAN))
    live_peer = packed[flags:, :SPAN].astype(jnp.float32)
    return jnp.where(ordered(first, live, live_peer, 1) > 0.5, 0.0, -1e30)


def probabilities(scale, queries, keys, bias):
    scores = dot(keys, queries, NT) * scale
    scores = jnp.concatenate([scores[:BLOCK] + bias[0:1], scores[BLOCK:] + bias[1:2]], axis=0)
    weights = jnp.exp(scores - jnp.max(scores, axis=0, keepdims=True))
    return weights * (1.0 / jnp.sum(weights, axis=0, keepdims=True))


def forward_kernel(scale, heads, place, q, k, v, packed, ids, count, context_out):
    first = place[0] == 0
    bias = block_bias(first, packed, ids, count)
    for h in range(heads):
        at, (queries, keys, values) = head_of(first, (q, k, v), packed, h)
        prob = probabilities(scale, queries, keys, bias)
        context_out[at, :] = dot(values, prob.astype(jnp.bfloat16), TN).astype(jnp.bfloat16)


def backward_kernel(
    scale, heads, place, q, k, v, packed, ids, count, cg_own, cg_peer, q_out, k_out, v_out, sent
):
    b16 = jnp.bfloat16
    first = place[0] == 0
    bias = block_bias(first, packed, ids, count)
    for h in range(heads):
        at, (queries, keys, values) = head_of(first, (q, k, v), packed, h)
        cg = (cg_own[at, :].astype(jnp.float32) + cg_peer[at, :].astype(jnp.float32)).astype(b16)
        prob = probabilities(scale, queries, keys, bias)
        dprob = dot(values, cg, NN)
        delta = jnp.sum(prob * dprob, axis=0, keepdims=True)
        dscore = (prob * (dprob - delta)).astype(b16)
        grads = (
            (dot(dscore, keys, TN) * scale).astype(b16),
            (dot(dscore, queries, NN) * scale).astype(b16),
            dot(prob.astype(b16), cg, NT).astype(b16),
        )
        for i, (grad, out) in enumerate(zip(grads, (q_out, k_out, v_out))):
            out[0, :, at] = jnp.where(first, grad[:SPAN], grad[SPAN:])
            sent[i, :, at] = jnp.where(first, grad[SPAN:], grad[:SPAN])


def place_kernel(place, received, q_in, k_in, v_in, q_out, k_out, v_out):
    for i, out in enumerate((q_out, k_out, v_out)):
        out[0] = received[i]


def projection_kernel(half_tiles, place, grads, weight, sent, kept):
    value = dot(weight[...], grads[0], NT).astype(jnp.bfloat16)

    @pl.when(pl.program_id(0) < half_tiles)
    def _():
        sent[...] = value

    @pl.when(pl.program_id(0) >= half_tiles)
    def _():
        kept[...] = value


def weight_kernel(left_at, straight_at, crossed_at, place, *refs):
    left, refs = refs[: len(left_at)], refs[len(left_at) :]
    straight, refs = refs[: len(straight_at)], refs[len(straight_at) :]
    crossed, refs = refs[: len(crossed_at)], refs[len(crossed_at) :]
    out, panel, right, left_done, right_done = refs[-5:]
    j = pl.program_id(0)
    depth, tile = left[0].shape[1], out.shape[1]
    per_half = crossed[1].shape[1] // tile

    def fetch(step, start):
        slot = lax.rem(step, 2)
        for half, (source, source_at) in enumerate(((straight, straight_at), (crossed, crossed_at))):

            @pl.when(step // per_half == half)
            def _():
                for i, (ref, at) in enumerate(zip(source, source_at)):
                    column = lax.rem(step, per_half) * tile
                    if i == 0:
                        column += place[1 + half] * per_half * tile
                    ref = ref if at is None else ref.at[at]
                    copy = pltpu.make_async_copy(
                        ref.at[:, pl.ds(pl.multiple_of(column, tile), tile)],
                        right.at[slot, pl.ds(i * depth, depth)],
                        right_done.at[slot, i],
                    )
                    copy.start() if start else copy.wait()

    def gather_left(start):
        for n, (ref, at) in enumerate(zip(left, left_at)):
            i = n // 2

            @pl.when(place[3] == n % 2)
            def _():
                copy = pltpu.make_async_copy(
                    ref if at is None else ref.at[at],
                    panel.at[:, pl.ds(i * depth, depth)],
                    left_done.at[i],
                )
                copy.start() if start else copy.wait()

    @pl.when(j == 0)
    def _():
        fetch(j, True)
        gather_left(True)

    @pl.when(j + 1 < pl.num_programs(0))
    def _():
        fetch(j + 1, True)

    fetch(j, False)

    @pl.when(j == 0)
    def _():
        gather_left(False)

    out[...] = dot(panel[...], right[lax.rem(j, 2)], NN)


def weight_rows(place, left, straight, crossed, held, shape):
    def split(entries):
        entries = [entry if isinstance(entry, tuple) else (entry, None) for entry in entries]
        return [array for array, _ in entries], [at for _, at in entries]

    count = len(left)
    left, left_at = split([entry for pair in left for entry in pair])
    straight, straight_at = split(straight)
    crossed, crossed_at = split(crossed)
    straight[0], crossed[0] = straight[0][0], crossed[0][0]
    rows, depth = left[0].shape
    columns = shape[1]
    tile = 512
    per_half = columns // 2 // tile
    hbm = pl.BlockSpec(memory_space=pl.ANY)
    inputs = [(array, hbm) for array in (*left, *straight, *crossed)]
    aliases = {}
    if held is not None:
        inputs.append((held, hbm))
        aliases = {len(inputs): 0}

    def to(j, p):
        return p[0], lax.rem(j, per_half) + jnp.where(j < per_half, p[1], p[2]) * per_half

    return call(
        lambda *refs: weight_kernel(left_at, straight_at, crossed_at, *refs),
        place,
        (2 * per_half,),
        inputs,
        [(shape, jnp.float32, pl.BlockSpec((rows, tile), to))],
        (
            2 * rows * depth * count * columns,
            4 * rows * columns + 2 * count * depth * (rows + columns),
            0,
        ),
        aliases,
        [
            pltpu.VMEM((rows, count * depth), jnp.bfloat16),
            pltpu.VMEM((2, count * depth, tile), jnp.bfloat16),
            pltpu.SemaphoreType.DMA((count,)),
            pltpu.SemaphoreType.DMA((2, count)),
        ],
    )[0]


def queue(axis, pairs, ordered_queue=True):
    arrived = []

    def send(value):
        if arrived and ordered_queue:
            value = lax.optimization_barrier((value, arrived[-1]))[0]
        arrived.append(lax.ppermute(value, axis, pairs))
        return arrived[-1]

    return send


def flipped(axis, bits, ordered_queue=True):
    return queue(axis, [(i, i ^ bits) for i in range(lax.axis_size(axis))], ordered_queue)


def middle_pairs():
    pairs = []
    for d in range(8):
        for core in range(2):
            other = (d ^ 6, core) if d // 2 in (1, 2) else (d, 1 - core)
            pairs.append((2 * d + core, 2 * other[0] + other[1]))
    return pairs


def pick_kernel(place, *refs):
    ends, middles, out, done = refs[:2], refs[2:4], refs[4], refs[5]
    for i in range(2):
        for chosen, source in ((0, ends[i]), (1, middles[i])):

            @pl.when(place[0] == chosen)
            def _():
                pltpu.make_async_copy(source, out.at[i], done.at[i]).start()

    for i in range(2):
        pltpu.make_async_copy(ends[i], out.at[i], done.at[i]).wait()


def paired(queries, key_states, value_states, out_grad, out_weight, align_ids, align_count):
    b16 = jnp.bfloat16
    i32 = jnp.int32
    scale = 1.0 / math.sqrt(HEAD_DIM)
    width = queries.shape[2]
    half = width // 2
    heads = half // HEAD_DIM
    rows = queries.shape[1]
    tokens, columns = out_grad.shape[1:]
    y = lax.axis_index("span").astype(i32)
    t = lax.axis_index("tensor").astype(i32)
    z = lax.axis_index("dp").astype(i32) // 2
    middle = (z == 1) | (z == 2)
    place = y[None]
    is_middle = middle.astype(i32)
    send_x, send_y, send_core = flipped("dp", 1), flipped("span", 1), flipped("tensor", 1, False)
    send_edge, send_middle = flipped("dp", 2), queue(("dp", "tensor"), middle_pairs())

    def whole(shape):
        return pl.BlockSpec(shape, lambda j, p: (0,) * len(shape))

    def half_of(which):
        return pl.BlockSpec((1, rows, half), lambda j, p: (0, 0, which(p[0])))

    def after(value, *others):
        return lax.optimization_barrier((value, *others))[0]

    own_half, peer_half = half_of(lambda y: y), half_of(lambda y: 1 - y)
    own = (queries, key_states, value_states)
    smem = pl.BlockSpec(memory_space=pltpu.SMEM)
    hbm = pl.BlockSpec(memory_space=pl.ANY)
    packed_shape = (3 * rows + FLAG_ROWS, half)
    (packed,) = call(
        prepare_kernel,
        place,
        (1,),
        [(v, peer_half) for v in own] + [(align_ids, smem), (align_count, smem)],
        [(packed_shape, b16, whole(packed_shape))],
        (0, 12 * rows * half, 0),
    )
    packed_sent = packed
    packed = send_y(packed)

    grad_half = lax.dynamic_slice_in_dim(out_grad[0], t * (columns // 2), columns // 2, axis=1)
    grad_half = after(grad_half, packed_sent)
    grad_x = send_x(grad_half)
    grad_1 = send_edge(grad_half)
    grad_2m = send_middle(grad_half)
    tile = 512
    half_tiles = half // tile
    whole_grad = pl.BlockSpec((1, tokens, columns), lambda j, p: (0, 0, 0))
    cg_sent, cg_own = call(
        lambda *refs: projection_kernel(half_tiles, *refs),
        place,
        (2 * half_tiles,),
        [
            (out_grad, whole_grad),
            (
                out_weight,
                pl.BlockSpec(
                    (tile, columns),
                    lambda j, p: (lax.rem(j + (1 - p[0]) * half_tiles, 2 * half_tiles), 0),
                ),
            ),
        ],
        [
            (
                (half, tokens),
                b16,
                pl.BlockSpec((tile, tokens), lambda j, p: (jnp.minimum(j, half_tiles - 1), 0)),
            ),
            (
                (half, tokens),
                b16,
                pl.BlockSpec((tile, tokens), lambda j, p: (jnp.maximum(j - half_tiles, 0), 0)),
            ),
        ],
        (2 * tokens * columns * width, 2 * columns * (tokens + width), 0),
    )

    own_in = [(v, own_half) for v in own]
    cg_peer = send_y(cg_sent)
    grad_1, grad_2m = lax.optimization_barrier((grad_1, grad_2m, cg_sent))[:2]
    grad_2e = send_edge(grad_2m)
    grad_3m = send_middle(grad_1)
    grad_1x = send_x(grad_1)
    packed_in = (after(packed, cg_sent), whole(packed_shape))
    (context,) = call(
        lambda *refs: forward_kernel(scale, heads, *refs),
        place,
        (1,),
        own_in + [packed_in, (align_ids, smem), (align_count, smem)],
        [((half, tokens), b16, whole((half, tokens)))],
        (heads * 2**25, 3 * MIB, heads * 2**16),
    )

    context_x = send_x(context)
    context_y = send_y(context)
    near_1 = send_edge(context)
    near_2m = send_middle(context)
    grad_3e = send_edge(grad_3m)
    near_2e = send_edge(near_2m)
    near_3m = send_middle(near_1)
    near_3e = send_edge(near_3m)
    def pick(ends, middles):
        shape = ends[0].shape
        return call(
            pick_kernel,
            is_middle[None],
            (1,),
            [(array, hbm) for array in (*ends, *middles)],
            [((2, *shape), b16, whole((2, *shape)))],
            (0, 8 * shape[0] * shape[1], 0),
            scratch=[pltpu.SemaphoreType.DMA((2,))],
        )[0]

    grad_p = pick((grad_2e, grad_3e), (grad_2m, grad_3m))
    near_p = pick((near_2e, near_3e), (near_2m, near_3m))
    grad_px = send_x(grad_p)
    diagonal = send_y(context_x)
    diagonal_1 = send_edge(diagonal)
    diagonal_2m = send_middle(diagonal)
    diagonal_2e = send_edge(diagonal_2m)
    diagonal_3m = send_middle(diagonal_1)
    diagonal_3e = send_edge(diagonal_3m)
    near_1x, near_1y = send_x(near_1), send_y(near_1)
    near_px, near_py = send_x(near_p), send_y(near_p)
    grad_1c = send_core(grad_1)
    grad_pc = send_core(grad_p)
    grad_xc = send_core(grad_x)
    grad_1xc = send_core(grad_1x)
    grad_pxc = send_core(grad_px)

    cg_shape = (half, tokens)
    full = (1, rows, width)
    sent_shape = (3, rows, half)
    *outs, sent = call(
        lambda *refs: backward_kernel(scale, heads, *refs),
        place,
        (1,),
        own_in
        + [packed_in, (align_ids, smem), (align_count, smem)]
        + [(cg_own, whole(cg_shape)), (cg_peer, whole(cg_shape))],
        [(full, b16, own_half)] * 3 + [(sent_shape, b16, whole(sent_shape))],
        (heads * 2**26, 5 * MIB, heads * 2**16),
    )
    received = send_y(sent)
    outs = call(
        place_kernel,
        place,
        (1,),
        [(received, whole(sent_shape))] + [(out, hbm) for out in outs],
        [(full, b16, peer_half)] * 3,
        (0, 12 * rows * half, 0),
        {2 + i: i for i in range(3)},
    )

    shape = (width, columns)
    def parts(first, second, pair, first_x, second_x, pair_x):
        return [first, second, (pair, 0), (pair, 1), first_x, second_x, (pair_x, 0), (pair_x, 1)]

    straight = parts(out_grad, grad_1, grad_p, grad_x, grad_1x, grad_px)
    crossed = parts(out_grad, grad_1c, grad_pc, grad_xc, grad_1xc, grad_pxc)
    near = [(c, c) for c in parts(context, near_1, near_p, context_x, near_1x, near_px)]
    far = [(c, c) for c in (context_y, near_1y, (near_py, 0), (near_py, 1), diagonal, diagonal_1)]
    far += [(diagonal_2e, diagonal_2m), (diagonal_3e, diagonal_3m)]
    near_place = jnp.stack([y, t, 1 - t, is_middle])
    far_place = jnp.stack([1 - y, t, 1 - t, is_middle])
    grad = weight_rows(near_place, near, straight, crossed, None, shape)
    *outs, grad = lax.optimization_barrier((*outs, grad))
    grad = weight_rows(far_place, far, straight, crossed, grad, shape)
    return (*outs, grad)


def shards(queries, key_states, value_states, out_grad, out_weight, align_ids, align_count):
    two_spans = lax.axis_size("span") == 2 and queries.shape[1] == SPAN == key_states.shape[1]
    if two_spans and lax.axis_size("dp") == 8 and lax.axis_size("tensor") == 2:
        return paired(
            queries, key_states, value_states, out_grad, out_weight, align_ids, align_count
        )
    f32 = jnp.float32
    b16 = jnp.bfloat16
    scale = 1.0 / math.sqrt(HEAD_DIM)
    local_width = queries.shape[2]
    local_heads = local_width // HEAD_DIM
    target_rows = queries.shape[1]
    source_rows = key_states.shape[1]
    span_number = target_rows // SPAN
    block_number = source_rows // BLOCK
    grad_rows = out_grad[0]
    context_grad = (
        lax.psum_scatter(
            lax.dot_general(
                grad_rows, out_weight, (((1,), (1,)), ((), ())), preferred_element_type=f32
            ).astype(jnp.bfloat16),
            "span",
            scatter_dimension=0,
            tiled=True,
        )
        .astype(jnp.float32)
        .astype(b16)
    )
    stacked = jnp.stack([key_states[0], value_states[0]])
    panel = with_halo(stacked, (("span", 1),), source_rows)
    position = lax.axis_index("span")
    local_ids = align_ids[0] - (position - 1) * block_number
    panel_blocks = panel.reshape(2, 3 * block_number, BLOCK, local_width)
    fetched = panel_blocks[:, local_ids]
    key_near = fetched[0].reshape(span_number, ALIGN * BLOCK, local_heads, HEAD_DIM)
    value_near = fetched[1].reshape(span_number, ALIGN * BLOCK, local_heads, HEAD_DIM)
    query_heads = queries[0].reshape(span_number, SPAN, local_heads, HEAD_DIM)
    live = (jnp.arange(ALIGN * BLOCK) // BLOCK)[None, :] < align_count[0][:, None]
    mask = live[:, None, None, :]
    scores = (
        jnp.einsum("nqhd,nkhd->nhqk", query_heads, key_near, preferred_element_type=f32) * scale
    )
    masked = jnp.where(mask, scores, -1e30)
    top = jnp.max(masked, axis=-1, keepdims=True)
    weights = jnp.where(mask, jnp.exp(masked - top), 0.0)
    prob = weights / jnp.sum(weights, axis=-1, keepdims=True)
    prob_half = prob.astype(b16)
    context = jnp.einsum(
        "nhqk,nkhd->nqhd", prob_half, value_near, preferred_element_type=f32
    ).astype(b16)
    grad_heads = context_grad.reshape(span_number, SPAN, local_heads, HEAD_DIM)
    dprob = jnp.einsum("nqhd,nkhd->nhqk", grad_heads, value_near, preferred_element_type=f32)
    delta = jnp.einsum("nqhd,nqhd->nhq", grad_heads, context, preferred_element_type=f32)[..., None]
    dscore = (prob * (dprob - delta)).astype(b16)
    query_grad = (
        jnp.einsum("nhqk,nkhd->nqhd", dscore, key_near, preferred_element_type=f32) * scale
    ).astype(b16)
    key_term = (
        jnp.einsum("nhqk,nqhd->nkhd", dscore, query_heads, preferred_element_type=f32) * scale
    )
    value_term = jnp.einsum("nhqk,nqhd->nkhd", prob_half, grad_heads, preferred_element_type=f32)
    slot_terms = jnp.stack([key_term, value_term]).reshape(
        2, span_number * ALIGN, BLOCK, local_width
    )
    flat_ids = local_ids.reshape(span_number * ALIGN)
    spread = (
        jnp.zeros((2, 3 * block_number, BLOCK, local_width), f32).at[:, flat_ids].add(slot_terms)
    )
    spread = spread.reshape(2, 3 * source_rows, local_width)
    lower_rim = spread[:, :source_rows].astype(b16)
    upper_rim = spread[:, 2 * source_rows :].astype(b16)
    from_above = shifted(lower_rim, "span", -1)
    from_below = shifted(upper_rim, "span", 1)
    summed = (
        spread[:, source_rows : 2 * source_rows] + from_above.astype(f32) + from_below.astype(f32)
    )
    pair_grad = summed.astype(b16)
    flat_context = context.reshape(target_rows, local_width)
    documents = lax.axis_size("dp")
    tokens = documents * grad_rows.shape[0]
    columns = grad_rows.shape[1]
    if tokens * (local_width + columns) <= 2 * local_width * columns:
        cores = lax.axis_size("tensor")
        share = grad_rows.shape[0] // cores
        own_share = lax.dynamic_slice_in_dim(
            grad_rows, lax.axis_index("tensor") * share, share, axis=0
        )
        all_grad = lax.all_gather(own_share, ("dp", "tensor"), axis=0, tiled=True)
        all_context = lax.all_gather(flat_context, ("dp", "span"), axis=0, tiled=True)
        weight_grad = lax.dot_general(
            all_context, all_grad, (((0,), (0,)), ((), ())), preferred_element_type=f32
        )
    else:
        gathered = lax.all_gather(flat_context, "span", axis=0, tiled=True)
        partial_grad = lax.dot_general(
            gathered, grad_rows, (((0,), (0,)), ((), ())), preferred_element_type=f32
        )
        weight_grad = lax.psum(partial_grad, "dp")
    query_out = query_grad.reshape(1, target_rows, local_width)
    return (query_out, pair_grad[0][None], pair_grad[1][None], weight_grad)


def solution(mesh):
    return jax.shard_map(
        shards,
        mesh=mesh,
        in_specs=(
            P("dp", "span", "tensor"),
            P("dp", "span", "tensor"),
            P("dp", "span", "tensor"),
            P("dp", None, "span"),
            P("tensor", "span"),
            P("dp", "span", None),
            P("dp", "span"),
        ),
        out_specs=(
            P("dp", "span", "tensor"),
            P("dp", "span", "tensor"),
            P("dp", "span", "tensor"),
            P("tensor", "span"),
        ),
        check_vma=False,
    )
```

```python
import math

import jax
import jax.numpy as jnp
from jax import lax
from jax.experimental import pallas as pl
from jax.experimental.pallas import tpu as pltpu
from jax.sharding import PartitionSpec as P

HEAD_DIM = 128
SPAN = 128
BLOCK = 128
ALIGN = 2


def with_halo(block, sides, width):
    for axis, dim in sides:
        count = lax.axis_size(axis)
        forward = [(i, i + 1) for i in range(count - 1)]
        backward = [(target, source) for source, target in forward]
        low = lax.ppermute(
            lax.slice_in_dim(block, block.shape[dim] - width, None, axis=dim), axis, forward
        )
        high = lax.ppermute(lax.slice_in_dim(block, 0, width, axis=dim), axis, backward)
        block = jnp.concatenate([low, block, high], axis=dim)
    return block


def shifted(value, axis, steps):
    count = lax.axis_size(axis)
    initial, last = (max(0, -steps), min(count, count - steps))
    return lax.ppermute(value, axis, [(source, source + steps) for source in range(initial, last)])


NT = (((1,), (1,)), ((), ()))
TN = (((0,), (0,)), ((), ()))
NN = (((1,), (0,)), ((), ()))
MIB = 2**20
FLAG_ROWS = 16


def dot(a, b, dims):
    return lax.dot_general(a, b, dims, preferred_element_type=jnp.float32)


def ordered(first, own, peer, axis):
    return jnp.where(
        first, jnp.concatenate([own, peer], axis=axis), jnp.concatenate([peer, own], axis=axis)
    )


def call(kernel, place, grid, inputs, outputs, cost, aliases=None, scratch=(), vmem=60):
    flops, moved, exps = cost
    return pl.pallas_call(
        kernel,
        grid_spec=pltpu.PrefetchScalarGridSpec(
            num_scalar_prefetch=1,
            grid=grid,
            in_specs=[spec for _, spec in inputs],
            out_specs=[spec for _, _, spec in outputs],
            scratch_shapes=list(scratch),
        ),
        out_shape=[jax.ShapeDtypeStruct(shape, dtype) for shape, dtype, _ in outputs],
        input_output_aliases=aliases or {},
        compiler_params=pltpu.CompilerParams(vmem_limit_bytes=vmem * MIB),
        cost_estimate=pl.CostEstimate(flops=flops, bytes_accessed=moved, transcendentals=exps),
    )(place, *[array for array, _ in inputs])


def live_flags(ids, count, shape):
    row = lax.broadcasted_iota(jnp.int32, shape, 0)
    found = jnp.zeros(shape, jnp.float32)
    for slot in range(ALIGN):
        alive = slot < count[0, 0]
        found += jnp.where((row == ids[0, 0, slot]) & alive, 1.0, 0.0)
    return found


def prepare_kernel(place, q, k, v, ids, count, packed):
    rows = q.shape[1]
    for i, ref in enumerate((q, k, v)):
        packed[i * rows : (i + 1) * rows] = ref[0]
    packed[3 * rows :] = live_flags(ids, count, (FLAG_ROWS, q.shape[2])).astype(jnp.bfloat16)


def head_of(first, own, packed, h):
    at = slice(h * HEAD_DIM, (h + 1) * HEAD_DIM)
    rows = own[0].shape[1]
    return at, [
        ordered(first, ref[0, :, at], packed[i * rows : (i + 1) * rows, at], 0)
        for i, ref in enumerate(own)
    ]


def block_bias(first, packed, ids, count):
    flags = packed.shape[0] - FLAG_ROWS
    live = live_flags(ids, count, (FLAG_ROWS, SPAN))
    live_peer = packed[flags:, :SPAN].astype(jnp.float32)
    return jnp.where(ordered(first, live, live_peer, 1) > 0.5, 0.0, -1e30)


def probabilities(scale, queries, keys, bias):
    scores = dot(keys, queries, NT) * scale
    scores = jnp.concatenate([scores[:BLOCK] + bias[0:1], scores[BLOCK:] + bias[1:2]], axis=0)
    weights = jnp.exp(scores - jnp.max(scores, axis=0, keepdims=True))
    return weights * (1.0 / jnp.sum(weights, axis=0, keepdims=True))


def forward_kernel(scale, heads, place, q, k, v, packed, ids, count, context_out):
    first = place[0] == 0
    bias = block_bias(first, packed, ids, count)
    for h in range(heads):
        at, (queries, keys, values) = head_of(first, (q, k, v), packed, h)
        prob = probabilities(scale, queries, keys, bias)
        context_out[at, :] = dot(values, prob.astype(jnp.bfloat16), TN).astype(jnp.bfloat16)


def backward_kernel(
    scale, heads, place, q, k, v, packed, ids, count, cg_own, cg_peer, q_out, k_out, v_out, sent
):
    b16 = jnp.bfloat16
    first = place[0] == 0
    bias = block_bias(first, packed, ids, count)
    for h in range(heads):
        at, (queries, keys, values) = head_of(first, (q, k, v), packed, h)
        cg = (cg_own[at, :].astype(jnp.float32) + cg_peer[at, :].astype(jnp.float32)).astype(b16)
        prob = probabilities(scale, queries, keys, bias)
        dprob = dot(values, cg, NN)
        delta = jnp.sum(prob * dprob, axis=0, keepdims=True)
        dscore = (prob * (dprob - delta)).astype(b16)
        grads = (
            (dot(dscore, keys, TN) * scale).astype(b16),
            (dot(dscore, queries, NN) * scale).astype(b16),
            dot(prob.astype(b16), cg, NT).astype(b16),
        )
        for i, (grad, out) in enumerate(zip(grads, (q_out, k_out, v_out))):
            out[0, :, at] = jnp.where(first, grad[:SPAN], grad[SPAN:])
            sent[i, :, at] = jnp.where(first, grad[SPAN:], grad[:SPAN])


def place_kernel(place, received, q_in, k_in, v_in, q_out, k_out, v_out):
    for i, out in enumerate((q_out, k_out, v_out)):
        out[0] = received[i]


def projection_kernel(half_tiles, place, grads, weight, sent, kept):
    value = dot(weight[...], grads[0], NT).astype(jnp.bfloat16)

    @pl.when(pl.program_id(0) < half_tiles)
    def _():
        sent[...] = value

    @pl.when(pl.program_id(0) >= half_tiles)
    def _():
        kept[...] = value


def weight_kernel(left_at, straight_at, crossed_at, per_half, add, place, *refs):
    left, refs = refs[: len(left_at)], refs[len(left_at) :]
    straight, refs = refs[: len(straight_at)], refs[len(straight_at) :]
    crossed, refs = refs[: len(crossed_at)], refs[len(crossed_at) :]
    out, panel, right, left_done, right_done = refs[-5:]
    j = pl.program_id(0)
    depth, tile = panel.shape[1] // len(straight), out.shape[1]

    def fetch(step, start):
        slot = lax.rem(step, 2)
        for half, (source, source_at) in enumerate(((straight, straight_at), (crossed, crossed_at))):

            @pl.when(step // per_half == half)
            def _():
                for i, (ref, at) in enumerate(zip(source, source_at)):
                    column = lax.rem(step, per_half) * tile
                    ref = ref if at is None else ref.at[at]
                    if ref.shape[1] > per_half * tile:
                        column += place[1 + half] * per_half * tile
                    copy = pltpu.make_async_copy(
                        ref.at[:, pl.ds(pl.multiple_of(column, tile), tile)],
                        right.at[slot, pl.ds(i * depth, depth)],
                        right_done.at[slot, i],
                    )
                    copy.start() if start else copy.wait()

    def gather_left(start):
        for n, (ref, at) in enumerate(zip(left, left_at)):
            i = n // 2

            @pl.when(place[3] == n % 2)
            def _():
                copy = pltpu.make_async_copy(
                    ref if at is None else ref.at[at],
                    panel.at[:, pl.ds(i * depth, depth)],
                    left_done.at[i],
                )
                copy.start() if start else copy.wait()

    @pl.when(j == 0)
    def _():
        fetch(j, True)
        gather_left(True)

    @pl.when(j + 1 < pl.num_programs(0))
    def _():
        fetch(j + 1, True)

    @pl.when(j == 0)
    def _():
        gather_left(False)

    fetch(j, False)
    value = dot(panel[...], right[lax.rem(j, 2)], NN)
    if add:
        value += refs[0][...].astype(jnp.float32)
    out[...] = value.astype(out.dtype)


def weight_rows(place, left, straight, crossed, part, held, shape):
    def split(entries):
        entries = [entry if isinstance(entry, tuple) else (entry, None) for entry in entries]
        return [array for array, _ in entries], [at for _, at in entries]

    count = len(left)
    left, left_at = split([entry for pair in left for entry in pair])
    straight, straight_at = split(straight)
    crossed, crossed_at = split(crossed)
    rows, depth = left[0].shape[-2:]
    tile = 512
    per_half = crossed[-1].shape[-1] // tile
    columns = 2 * per_half * tile
    hbm = pl.BlockSpec(memory_space=pl.ANY)
    inputs = [(array, hbm) for array in (*left, *straight, *crossed)]

    def column(j, p):
        return lax.rem(j, per_half) + jnp.where(j < per_half, p[1], p[2]) * per_half

    alone = pl.BlockSpec((rows, tile), lambda j, p: (0, column(j, p)))
    block = pl.BlockSpec((rows, tile), lambda j, p: (p[0], column(j, p)))
    if part is not None:
        inputs.append((part, alone))
    aliases = {}
    if held is not None:
        inputs.append((held, hbm))
        aliases = {len(inputs): 0}
    if shape is None:
        output = ((rows, columns), jnp.bfloat16, alone)
    else:
        output = (shape, jnp.float32, block)
    return call(
        lambda *refs: weight_kernel(
            left_at, straight_at, crossed_at, per_half, part is not None, *refs
        ),
        place,
        (2 * per_half,),
        inputs,
        [output],
        (
            2 * rows * depth * count * columns,
            4 * rows * columns + 2 * count * depth * (rows + columns),
            0,
        ),
        aliases,
        [
            pltpu.VMEM((rows, count * depth), jnp.bfloat16),
            pltpu.VMEM((2, count * depth, tile), jnp.bfloat16),
            pltpu.SemaphoreType.DMA((count,)),
            pltpu.SemaphoreType.DMA((2, count)),
        ],
    )[0]


def after(value, others):
    return lax.optimization_barrier((value, *others))[0] if others else value


def queue(axis, pairs, in_order=True):
    arrived = []

    def send(value, *others):
        if in_order:
            others += tuple(arrived[-1:])
        arrived.append(lax.ppermute(after(value, others), axis, pairs))
        return arrived[-1]

    return send


def flipped(axis, bits, in_order=True):
    return queue(axis, [(i, i ^ bits) for i in range(lax.axis_size(axis))], in_order)


def middle_pairs():
    pairs = []
    for d in range(8):
        for core in range(2):
            other = (d ^ 6, core) if d // 2 in (1, 2) else (d, 1 - core)
            pairs.append((2 * d + core, 2 * other[0] + other[1]))
    return pairs


def pick_kernel(place, *refs):
    ends, middles, out, done = refs[:2], refs[2:4], refs[4], refs[5]
    for i in range(2):
        for chosen, source in ((0, ends[i]), (1, middles[i])):

            @pl.when(place[0] == chosen)
            def _():
                pltpu.make_async_copy(source, out.at[i], done.at[i]).start()

    for i in range(2):
        pltpu.make_async_copy(ends[i], out.at[i], done.at[i]).wait()


def paired(queries, key_states, value_states, out_grad, out_weight, align_ids, align_count):
    b16 = jnp.bfloat16
    i32 = jnp.int32
    scale = 1.0 / math.sqrt(HEAD_DIM)
    width = queries.shape[2]
    half = width // 2
    heads = half // HEAD_DIM
    rows = queries.shape[1]
    tokens, columns = out_grad.shape[1:]
    y = lax.axis_index("span").astype(i32)
    t = lax.axis_index("tensor").astype(i32)
    z = lax.axis_index("dp").astype(i32) // 2
    middle = (z == 1) | (z == 2)
    place = y[None]
    is_middle = middle.astype(i32)
    send_x, send_y, send_core = flipped("dp", 1), flipped("span", 1), flipped("tensor", 1, False)
    send_edge, send_middle = flipped("dp", 2), queue(("dp", "tensor"), middle_pairs())

    def whole(shape):
        return pl.BlockSpec(shape, lambda j, p: (0,) * len(shape))

    def half_of(which, parts=1):
        return pl.BlockSpec((1, rows, half // parts), lambda j, p: (0, 0, which(p[0]) * parts + j))

    own_half, peer_half = half_of(lambda y: y), half_of(lambda y: 1 - y)
    own = (queries, key_states, value_states)
    smem = pl.BlockSpec(memory_space=pltpu.SMEM)
    hbm = pl.BlockSpec(memory_space=pl.ANY)
    packed_shape = (3 * rows + FLAG_ROWS, half)
    (packed,) = call(
        prepare_kernel,
        place,
        (1,),
        [(v, peer_half) for v in own] + [(align_ids, smem), (align_count, smem)],
        [(packed_shape, b16, whole(packed_shape))],
        (0, 12 * rows * half, 0),
    )
    packed_sent = packed
    packed = send_y(packed)

    grad_half = lax.dynamic_slice_in_dim(out_grad[0], t * (columns // 2), columns // 2, axis=1)
    grad_half = after(grad_half, [packed_sent])
    grad_x = send_x(grad_half)
    grad_1 = send_edge(grad_half)
    grad_2m = send_middle(grad_half)
    tile = 512
    half_tiles = half // tile
    whole_grad = pl.BlockSpec((1, tokens, columns), lambda j, p: (0, 0, 0))
    cg_sent, cg_own = call(
        lambda *refs: projection_kernel(half_tiles, *refs),
        place,
        (2 * half_tiles,),
        [
            (out_grad, whole_grad),
            (
                out_weight,
                pl.BlockSpec(
                    (tile, columns),
                    lambda j, p: (lax.rem(j + (1 - p[0]) * half_tiles, 2 * half_tiles), 0),
                ),
            ),
        ],
        [
            (
                (half, tokens),
                b16,
                pl.BlockSpec((tile, tokens), lambda j, p: (jnp.minimum(j, half_tiles - 1), 0)),
            ),
            (
                (half, tokens),
                b16,
                pl.BlockSpec((tile, tokens), lambda j, p: (jnp.maximum(j - half_tiles, 0), 0)),
            ),
        ],
        (2 * tokens * columns * width, 2 * columns * (tokens + width), 0),
    )

    groups = 2
    heads //= groups
    own_in = [(v, half_of(lambda y: y, groups)) for v in own]
    grad_2e = send_edge(grad_2m, cg_sent, grad_x, packed)
    grad_3m = send_middle(grad_1, cg_sent, grad_x, packed)
    grad_1x = send_x(grad_1, packed)
    cg_peer = send_y(cg_sent)
    group = half // groups
    packed_block = pl.BlockSpec((packed_shape[0], group), lambda j, p: (0, j))
    packed_in = (after(packed, [cg_sent]), packed_block)
    feature_block = pl.BlockSpec((group, tokens), lambda j, p: (j, 0))
    (context,) = call(
        lambda *refs: forward_kernel(scale, heads, *refs),
        place,
        (groups,),
        own_in + [packed_in, (align_ids, smem), (align_count, smem)],
        [((half, tokens), b16, feature_block)],
        (groups * heads * 2**25, 3 * MIB, groups * heads * 2**16),
    )

    def pick(ends, middles):
        shape = ends[0].shape
        return call(
            pick_kernel,
            is_middle[None],
            (1,),
            [(array, hbm) for array in (*ends, *middles)],
            [((2, *shape), b16, whole((2, *shape)))],
            (0, 8 * shape[0] * shape[1], 0),
            scratch=[pltpu.SemaphoreType.DMA((2,))],
        )[0]

    context_x = send_x(context)
    context_y = send_y(context)
    near_1 = send_edge(context, grad_1x, cg_peer)
    near_2m = send_middle(context, cg_peer)
    grad_3e = send_edge(grad_3m, context_x)
    near_3m = send_middle(near_1)
    diagonal = send_y(context_x)
    near_1x = send_x(near_1)
    full = (1, rows, width)
    sent_shape = (3, rows, half)
    *outs, sent = call(
        lambda *refs: backward_kernel(scale, heads, *refs),
        place,
        (groups,),
        own_in
        + [packed_in, (align_ids, smem), (align_count, smem)]
        + [(cg_own, feature_block), (cg_peer, feature_block)],
        [(full, b16, half_of(lambda y: y, groups))] * 3
        + [(sent_shape, b16, pl.BlockSpec((3, rows, group), lambda j, p: (0, 0, j)))],
        (groups * heads * 2**26, 5 * MIB, groups * heads * 2**16),
    )
    near_2e = send_edge(near_2m, near_1x, diagonal, sent)
    grad_p = pick((grad_2e, grad_3e), (grad_2m, grad_3m))
    grad_px = send_x(grad_p)
    near_1y = send_y(near_1)
    near_3e = send_edge(near_3m, near_1y)
    near_p = pick((near_2e, near_3e), (near_2m, near_3m))
    near_px = send_x(near_p)
    near_py = send_y(near_p)
    received = send_y(sent)
    diagonal_1 = send_edge(diagonal, grad_px)
    diagonal_2m = send_middle(diagonal)
    diagonal_2e = send_edge(diagonal_2m)
    diagonal_3m = send_middle(diagonal_1)
    grad_1c = send_core(grad_1)
    grad_pc = send_core(grad_p)
    grad_xc = send_core(grad_x)
    grad_1xc = send_core(grad_1x)
    grad_pxc = send_core(grad_px)

    outs = call(
        place_kernel,
        place,
        (1,),
        [(received, whole(sent_shape))] + [(out, hbm) for out in outs],
        [(full, b16, peer_half)] * 3,
        (0, 12 * rows * half, 0),
        {2 + i: i for i in range(3)},
    )

    shape = (width, columns)
    def parts(first, second, pair, first_x, second_x, pair_x):
        return [first, second, (pair, 0), (pair, 1), first_x, second_x, (pair_x, 0), (pair_x, 1)]

    straight = parts((out_grad, 0), grad_1, grad_p, grad_x, grad_1x, grad_px)
    crossed = parts((out_grad, 0), grad_1c, grad_pc, grad_xc, grad_1xc, grad_pxc)
    near = [(c, c) for c in parts(context, near_1, near_p, context_x, near_1x, near_px)]
    near_place = jnp.stack([y, t, 1 - t, is_middle])
    far_place = jnp.stack([1 - y, t, 1 - t, is_middle])
    early = len(near) - 2
    part = weight_rows(
        near_place, near[:early], straight[:early], crossed[:early], None, None, None
    )
    diagonal_3e = send_edge(diagonal_3m, part)
    far = [(c, c) for c in (context_y, near_1y, (near_py, 0), (near_py, 1), diagonal, diagonal_1)]
    far += [(diagonal_2e, diagonal_2m), (diagonal_3e, diagonal_3m)]
    grad = weight_rows(
        near_place, near[early:], straight[early:], crossed[early:], part, None, shape
    )
    grad = weight_rows(far_place, far, straight, crossed, None, grad, shape)
    return (*outs, grad)


def shards(queries, key_states, value_states, out_grad, out_weight, align_ids, align_count):
    two_spans = lax.axis_size("span") == 2 and queries.shape[1] == SPAN == key_states.shape[1]
    if two_spans and lax.axis_size("dp") == 8 and lax.axis_size("tensor") == 2:
        return paired(
            queries, key_states, value_states, out_grad, out_weight, align_ids, align_count
        )
    f32 = jnp.float32
    b16 = jnp.bfloat16
    scale = 1.0 / math.sqrt(HEAD_DIM)
    local_width = queries.shape[2]
    local_heads = local_width // HEAD_DIM
    target_rows = queries.shape[1]
    source_rows = key_states.shape[1]
    span_number = target_rows // SPAN
    block_number = source_rows // BLOCK
    grad_rows = out_grad[0]
    context_grad = (
        lax.psum_scatter(
            lax.dot_general(
                grad_rows, out_weight, (((1,), (1,)), ((), ())), preferred_element_type=f32
            ).astype(jnp.bfloat16),
            "span",
            scatter_dimension=0,
            tiled=True,
        )
        .astype(jnp.float32)
        .astype(b16)
    )
    stacked = jnp.stack([key_states[0], value_states[0]])
    panel = with_halo(stacked, (("span", 1),), source_rows)
    position = lax.axis_index("span")
    local_ids = align_ids[0] - (position - 1) * block_number
    panel_blocks = panel.reshape(2, 3 * block_number, BLOCK, local_width)
    fetched = panel_blocks[:, local_ids]
    key_near = fetched[0].reshape(span_number, ALIGN * BLOCK, local_heads, HEAD_DIM)
    value_near = fetched[1].reshape(span_number, ALIGN * BLOCK, local_heads, HEAD_DIM)
    query_heads = queries[0].reshape(span_number, SPAN, local_heads, HEAD_DIM)
    live = (jnp.arange(ALIGN * BLOCK) // BLOCK)[None, :] < align_count[0][:, None]
    mask = live[:, None, None, :]
    scores = (
        jnp.einsum("nqhd,nkhd->nhqk", query_heads, key_near, preferred_element_type=f32) * scale
    )
    masked = jnp.where(mask, scores, -1e30)
    top = jnp.max(masked, axis=-1, keepdims=True)
    weights = jnp.where(mask, jnp.exp(masked - top), 0.0)
    prob = weights / jnp.sum(weights, axis=-1, keepdims=True)
    prob_half = prob.astype(b16)
    context = jnp.einsum(
        "nhqk,nkhd->nqhd", prob_half, value_near, preferred_element_type=f32
    ).astype(b16)
    grad_heads = context_grad.reshape(span_number, SPAN, local_heads, HEAD_DIM)
    dprob = jnp.einsum("nqhd,nkhd->nhqk", grad_heads, value_near, preferred_element_type=f32)
    delta = jnp.einsum("nqhd,nqhd->nhq", grad_heads, context, preferred_element_type=f32)[..., None]
    dscore = (prob * (dprob - delta)).astype(b16)
    query_grad = (
        jnp.einsum("nhqk,nkhd->nqhd", dscore, key_near, preferred_element_type=f32) * scale
    ).astype(b16)
    key_term = (
        jnp.einsum("nhqk,nqhd->nkhd", dscore, query_heads, preferred_element_type=f32) * scale
    )
    value_term = jnp.einsum("nhqk,nqhd->nkhd", prob_half, grad_heads, preferred_element_type=f32)
    slot_terms = jnp.stack([key_term, value_term]).reshape(
        2, span_number * ALIGN, BLOCK, local_width
    )
    flat_ids = local_ids.reshape(span_number * ALIGN)
    spread = (
        jnp.zeros((2, 3 * block_number, BLOCK, local_width), f32).at[:, flat_ids].add(slot_terms)
    )
    spread = spread.reshape(2, 3 * source_rows, local_width)
    lower_rim = spread[:, :source_rows].astype(b16)
    upper_rim = spread[:, 2 * source_rows :].astype(b16)
    from_above = shifted(lower_rim, "span", -1)
    from_below = shifted(upper_rim, "span", 1)
    summed = (
        spread[:, source_rows : 2 * source_rows] + from_above.astype(f32) + from_below.astype(f32)
    )
    pair_grad = summed.astype(b16)
    flat_context = context.reshape(target_rows, local_width)
    documents = lax.axis_size("dp")
    tokens = documents * grad_rows.shape[0]
    columns = grad_rows.shape[1]
    if tokens * (local_width + columns) <= 2 * local_width * columns:
        cores = lax.axis_size("tensor")
        share = grad_rows.shape[0] // cores
        own_share = lax.dynamic_slice_in_dim(
            grad_rows, lax.axis_index("tensor") * share, share, axis=0
        )
        all_grad = lax.all_gather(own_share, ("dp", "tensor"), axis=0, tiled=True)
        all_context = lax.all_gather(flat_context, ("dp", "span"), axis=0, tiled=True)
        weight_grad = lax.dot_general(
            all_context, all_grad, (((0,), (0,)), ((), ())), preferred_element_type=f32
        )
    else:
        gathered = lax.all_gather(flat_context, "span", axis=0, tiled=True)
        partial_grad = lax.dot_general(
            gathered, grad_rows, (((0,), (0,)), ((), ())), preferred_element_type=f32
        )
        weight_grad = lax.psum(partial_grad, "dp")
    query_out = query_grad.reshape(1, target_rows, local_width)
    return (query_out, pair_grad[0][None], pair_grad[1][None], weight_grad)


def solution(mesh):
    return jax.shard_map(
        shards,
        mesh=mesh,
        in_specs=(
            P("dp", "span", "tensor"),
            P("dp", "span", "tensor"),
            P("dp", "span", "tensor"),
            P("dp", None, "span"),
            P("tensor", "span"),
            P("dp", "span", None),
            P("dp", "span"),
        ),
        out_specs=(
            P("dp", "span", "tensor"),
            P("dp", "span", "tensor"),
            P("dp", "span", "tensor"),
            P("tensor", "span"),
        ),
        check_vma=False,
    )
```

```python
import math

import jax
import jax.numpy as jnp
from jax import lax
from jax.experimental import pallas as pl
from jax.experimental.pallas import tpu as pltpu
from jax.sharding import PartitionSpec as P

HEAD_DIM = 128
SPAN = 128
BLOCK = 128
ALIGN = 2


def with_halo(block, sides, width):
    for axis, dim in sides:
        count = lax.axis_size(axis)
        forward = [(i, i + 1) for i in range(count - 1)]
        backward = [(target, source) for source, target in forward]
        low = lax.ppermute(
            lax.slice_in_dim(block, block.shape[dim] - width, None, axis=dim), axis, forward
        )
        high = lax.ppermute(lax.slice_in_dim(block, 0, width, axis=dim), axis, backward)
        block = jnp.concatenate([low, block, high], axis=dim)
    return block


def shifted(value, axis, steps):
    count = lax.axis_size(axis)
    initial, last = (max(0, -steps), min(count, count - steps))
    return lax.ppermute(value, axis, [(source, source + steps) for source in range(initial, last)])


NT = (((1,), (1,)), ((), ()))
TN = (((0,), (0,)), ((), ()))
NN = (((1,), (0,)), ((), ()))
MIB = 2**20
FLAG_ROWS = 16


def dot(a, b, dims):
    return lax.dot_general(a, b, dims, preferred_element_type=jnp.float32)


def ordered(first, own, peer, axis):
    return jnp.where(
        first, jnp.concatenate([own, peer], axis=axis), jnp.concatenate([peer, own], axis=axis)
    )


def call(kernel, place, grid, inputs, outputs, cost, aliases=None, scratch=(), vmem=60):
    flops, moved, exps = cost
    return pl.pallas_call(
        kernel,
        grid_spec=pltpu.PrefetchScalarGridSpec(
            num_scalar_prefetch=1,
            grid=grid,
            in_specs=[spec for _, spec in inputs],
            out_specs=[spec for _, _, spec in outputs],
            scratch_shapes=list(scratch),
        ),
        out_shape=[jax.ShapeDtypeStruct(shape, dtype) for shape, dtype, _ in outputs],
        input_output_aliases=aliases or {},
        compiler_params=pltpu.CompilerParams(vmem_limit_bytes=vmem * MIB),
        cost_estimate=pl.CostEstimate(flops=flops, bytes_accessed=moved, transcendentals=exps),
    )(place, *[array for array, _ in inputs])


def live_flags(ids, count, shape):
    row = lax.broadcasted_iota(jnp.int32, shape, 0)
    found = jnp.zeros(shape, jnp.float32)
    for slot in range(ALIGN):
        alive = slot < count[0, 0]
        found += jnp.where((row == ids[0, 0, slot]) & alive, 1.0, 0.0)
    return found


def prepare_kernel(place, q, k, v, ids, count, packed):
    rows = q.shape[1]
    for i, ref in enumerate((q, k, v)):
        packed[i * rows : (i + 1) * rows] = ref[0]
    packed[3 * rows :] = live_flags(ids, count, (FLAG_ROWS, q.shape[2])).astype(jnp.bfloat16)


def head_of(first, own, packed, h):
    at = slice(h * HEAD_DIM, (h + 1) * HEAD_DIM)
    rows = own[0].shape[1]
    return at, [
        ordered(first, ref[0, :, at], packed[i * rows : (i + 1) * rows, at], 0)
        for i, ref in enumerate(own)
    ]


def block_bias(first, packed, ids, count):
    flags = packed.shape[0] - FLAG_ROWS
    live = live_flags(ids, count, (FLAG_ROWS, SPAN))
    live_peer = packed[flags:, :SPAN].astype(jnp.float32)
    return jnp.where(ordered(first, live, live_peer, 1) > 0.5, 0.0, -1e30)


def probabilities(scale, queries, keys, bias):
    scores = dot(keys, queries, NT) * scale
    scores = jnp.concatenate([scores[:BLOCK] + bias[0:1], scores[BLOCK:] + bias[1:2]], axis=0)
    weights = jnp.exp(scores - jnp.max(scores, axis=0, keepdims=True))
    return weights * (1.0 / jnp.sum(weights, axis=0, keepdims=True))


def forward_kernel(scale, heads, place, q, k, v, packed, ids, count, context_out):
    first = place[0] == 0
    bias = block_bias(first, packed, ids, count)
    for h in range(heads):
        at, (queries, keys, values) = head_of(first, (q, k, v), packed, h)
        prob = probabilities(scale, queries, keys, bias)
        context_out[at, :] = dot(values, prob.astype(jnp.bfloat16), TN).astype(jnp.bfloat16)


def backward_kernel(
    scale, heads, place, q, k, v, packed, ids, count, cg_own, cg_peer, q_out, k_out, v_out, sent
):
    b16 = jnp.bfloat16
    first = place[0] == 0
    bias = block_bias(first, packed, ids, count)
    for h in range(heads):
        at, (queries, keys, values) = head_of(first, (q, k, v), packed, h)
        cg = (cg_own[at, :].astype(jnp.float32) + cg_peer[at, :].astype(jnp.float32)).astype(b16)
        prob = probabilities(scale, queries, keys, bias)
        dprob = dot(values, cg, NN)
        delta = jnp.sum(prob * dprob, axis=0, keepdims=True)
        dscore = (prob * (dprob - delta)).astype(b16)
        grads = (
            (dot(dscore, keys, TN) * scale).astype(b16),
            (dot(dscore, queries, NN) * scale).astype(b16),
            dot(prob.astype(b16), cg, NT).astype(b16),
        )
        for i, (grad, out) in enumerate(zip(grads, (q_out, k_out, v_out))):
            out[0, :, at] = jnp.where(first, grad[:SPAN], grad[SPAN:])
            sent[i, :, at] = jnp.where(first, grad[SPAN:], grad[:SPAN])


def place_kernel(place, received, q_in, k_in, v_in, q_out, k_out, v_out):
    for i, out in enumerate((q_out, k_out, v_out)):
        out[0] = received[i]


def projection_kernel(half_tiles, place, grads, weight, sent, kept):
    value = dot(weight[...], grads[0], NT).astype(jnp.bfloat16)

    @pl.when(pl.program_id(0) < half_tiles)
    def _():
        sent[...] = value

    @pl.when(pl.program_id(0) >= half_tiles)
    def _():
        kept[...] = value


def weight_kernel(left_at, straight_at, crossed_at, per_half, add, place, *refs):
    left, refs = refs[: len(left_at)], refs[len(left_at) :]
    straight, refs = refs[: len(straight_at)], refs[len(straight_at) :]
    crossed, refs = refs[: len(crossed_at)], refs[len(crossed_at) :]
    out, panel, right, left_done, right_done = refs[-5:]
    j = pl.program_id(0)
    depth, tile = panel.shape[1] // len(straight), out.shape[1]

    def fetch(step, start):
        slot = lax.rem(step, 2)
        for half, (source, source_at) in enumerate(((straight, straight_at), (crossed, crossed_at))):

            @pl.when(step // per_half == half)
            def _():
                for i, (ref, at) in enumerate(zip(source, source_at)):
                    column = lax.rem(step, per_half) * tile
                    ref = ref if at is None else ref.at[at]
                    if ref.shape[1] > per_half * tile:
                        column += place[1 + half] * per_half * tile
                    copy = pltpu.make_async_copy(
                        ref.at[:, pl.ds(pl.multiple_of(column, tile), tile)],
                        right.at[slot, pl.ds(i * depth, depth)],
                        right_done.at[slot, i],
                    )
                    copy.start() if start else copy.wait()

    def gather_left(start):
        for n, (ref, at) in enumerate(zip(left, left_at)):
            i = n // 2

            @pl.when(place[3] == n % 2)
            def _():
                copy = pltpu.make_async_copy(
                    ref if at is None else ref.at[at],
                    panel.at[:, pl.ds(i * depth, depth)],
                    left_done.at[i],
                )
                copy.start() if start else copy.wait()

    @pl.when(j == 0)
    def _():
        fetch(j, True)
        gather_left(True)

    @pl.when(j + 1 < pl.num_programs(0))
    def _():
        fetch(j + 1, True)

    @pl.when(j == 0)
    def _():
        gather_left(False)

    fetch(j, False)
    value = dot(panel[...], right[lax.rem(j, 2)], NN)
    if add:
        value += refs[0][...].astype(jnp.float32)
    out[...] = value.astype(out.dtype)


def weight_rows(place, left, straight, crossed, part, held, shape):
    def split(entries):
        entries = [entry if isinstance(entry, tuple) else (entry, None) for entry in entries]
        return [array for array, _ in entries], [at for _, at in entries]

    count = len(left)
    left, left_at = split([entry for pair in left for entry in pair])
    straight, straight_at = split(straight)
    crossed, crossed_at = split(crossed)
    rows, depth = left[0].shape[-2:]
    tile = 512
    per_half = crossed[-1].shape[-1] // tile
    columns = 2 * per_half * tile
    hbm = pl.BlockSpec(memory_space=pl.ANY)
    inputs = [(array, hbm) for array in (*left, *straight, *crossed)]

    def column(j, p):
        return lax.rem(j, per_half) + jnp.where(j < per_half, p[1], p[2]) * per_half

    alone = pl.BlockSpec((rows, tile), lambda j, p: (0, column(j, p)))
    block = pl.BlockSpec((rows, tile), lambda j, p: (p[0], column(j, p)))
    if part is not None:
        inputs.append((part, alone))
    aliases = {}
    if held is not None:
        inputs.append((held, hbm))
        aliases = {len(inputs): 0}
    if shape is None:
        output = ((rows, columns), jnp.bfloat16, alone)
    else:
        output = (shape, jnp.float32, block)
    return call(
        lambda *refs: weight_kernel(
            left_at, straight_at, crossed_at, per_half, part is not None, *refs
        ),
        place,
        (2 * per_half,),
        inputs,
        [output],
        (
            2 * rows * depth * count * columns,
            4 * rows * columns + 2 * count * depth * (rows + columns),
            0,
        ),
        aliases,
        [
            pltpu.VMEM((rows, count * depth), jnp.bfloat16),
            pltpu.VMEM((2, count * depth, tile), jnp.bfloat16),
            pltpu.SemaphoreType.DMA((count,)),
            pltpu.SemaphoreType.DMA((2, count)),
        ],
    )[0]


def after(value, others):
    return lax.optimization_barrier((value, *others))[0] if others else value


def queue(axis, pairs, in_order=True):
    arrived = []

    def send(value, *others):
        if in_order:
            others += tuple(arrived[-1:])
        arrived.append(lax.ppermute(after(value, others), axis, pairs))
        return arrived[-1]

    return send


def flipped(axis, bits, in_order=True):
    return queue(axis, [(i, i ^ bits) for i in range(lax.axis_size(axis))], in_order)


def middle_pairs():
    pairs = []
    for d in range(8):
        for core in range(2):
            other = (d ^ 6, core) if d // 2 in (1, 2) else (d, 1 - core)
            pairs.append((2 * d + core, 2 * other[0] + other[1]))
    return pairs


def pick_kernel(place, *refs):
    ends, middles, out, done = refs[:2], refs[2:4], refs[4], refs[5]
    for i in range(2):
        for chosen, source in ((0, ends[i]), (1, middles[i])):

            @pl.when(place[0] == chosen)
            def _():
                pltpu.make_async_copy(source, out.at[i], done.at[i]).start()

    for i in range(2):
        pltpu.make_async_copy(ends[i], out.at[i], done.at[i]).wait()


def paired(queries, key_states, value_states, out_grad, out_weight, align_ids, align_count):
    b16 = jnp.bfloat16
    i32 = jnp.int32
    scale = 1.0 / math.sqrt(HEAD_DIM)
    width = queries.shape[2]
    half = width // 2
    heads = half // HEAD_DIM
    rows = queries.shape[1]
    tokens, columns = out_grad.shape[1:]
    y = lax.axis_index("span").astype(i32)
    t = lax.axis_index("tensor").astype(i32)
    z = lax.axis_index("dp").astype(i32) // 2
    middle = (z == 1) | (z == 2)
    place = y[None]
    is_middle = middle.astype(i32)
    send_x, send_y, send_core = flipped("dp", 1), flipped("span", 1), flipped("tensor", 1, False)
    send_edge, send_middle = flipped("dp", 2), queue(("dp", "tensor"), middle_pairs())

    def whole(shape):
        return pl.BlockSpec(shape, lambda j, p: (0,) * len(shape))

    def half_of(which, parts=1):
        return pl.BlockSpec((1, rows, half // parts), lambda j, p: (0, 0, which(p[0]) * parts + j))

    own_half, peer_half = half_of(lambda y: y), half_of(lambda y: 1 - y)
    own = (queries, key_states, value_states)
    smem = pl.BlockSpec(memory_space=pltpu.SMEM)
    hbm = pl.BlockSpec(memory_space=pl.ANY)
    packed_shape = (3 * rows + FLAG_ROWS, half)
    (packed,) = call(
        prepare_kernel,
        place,
        (1,),
        [(v, peer_half) for v in own] + [(align_ids, smem), (align_count, smem)],
        [(packed_shape, b16, whole(packed_shape))],
        (0, 12 * rows * half, 0),
    )
    packed_sent = packed
    packed = send_y(packed)

    grad_half = lax.dynamic_slice_in_dim(out_grad[0], t * (columns // 2), columns // 2, axis=1)
    grad_half = after(grad_half, [packed_sent])
    grad_x = send_x(grad_half)
    grad_1 = send_edge(grad_half)
    grad_2m = send_middle(grad_half)
    tile = 512
    half_tiles = half // tile
    whole_grad = pl.BlockSpec((1, tokens, columns), lambda j, p: (0, 0, 0))
    cg_sent, cg_own = call(
        lambda *refs: projection_kernel(half_tiles, *refs),
        place,
        (2 * half_tiles,),
        [
            (out_grad, whole_grad),
            (
                out_weight,
                pl.BlockSpec(
                    (tile, columns),
                    lambda j, p: (lax.rem(j + (1 - p[0]) * half_tiles, 2 * half_tiles), 0),
                ),
            ),
        ],
        [
            (
                (half, tokens),
                b16,
                pl.BlockSpec((tile, tokens), lambda j, p: (jnp.minimum(j, half_tiles - 1), 0)),
            ),
            (
                (half, tokens),
                b16,
                pl.BlockSpec((tile, tokens), lambda j, p: (jnp.maximum(j - half_tiles, 0), 0)),
            ),
        ],
        (2 * tokens * columns * width, 2 * columns * (tokens + width), 0),
    )

    groups = 2
    heads //= groups
    own_in = [(v, half_of(lambda y: y, groups)) for v in own]
    grad_2e = send_edge(grad_2m, cg_sent, grad_x)
    grad_3m = send_middle(grad_1, cg_sent, grad_x)
    grad_1x = send_x(grad_1, packed)
    cg_peer = send_y(cg_sent)
    group = half // groups
    packed_block = pl.BlockSpec((packed_shape[0], group), lambda j, p: (0, j))
    packed_in = (after(packed, [cg_sent]), packed_block)
    feature_block = pl.BlockSpec((group, tokens), lambda j, p: (j, 0))
    (context,) = call(
        lambda *refs: forward_kernel(scale, heads, *refs),
        place,
        (groups,),
        own_in + [packed_in, (align_ids, smem), (align_count, smem)],
        [((half, tokens), b16, feature_block)],
        (groups * heads * 2**25, 3 * MIB, groups * heads * 2**16),
    )

    def pick(ends, middles):
        shape = ends[0].shape
        return call(
            pick_kernel,
            is_middle[None],
            (1,),
            [(array, hbm) for array in (*ends, *middles)],
            [((2, *shape), b16, whole((2, *shape)))],
            (0, 8 * shape[0] * shape[1], 0),
            scratch=[pltpu.SemaphoreType.DMA((2,))],
        )[0]

    context_x = send_x(context)
    context_y = send_y(context)
    near_1 = send_edge(context, grad_1x, cg_peer)
    near_2m = send_middle(context, cg_peer)
    grad_3e = send_edge(grad_3m, context_x)
    near_3m = send_middle(near_1)
    diagonal = send_y(context_x)
    near_1x = send_x(near_1)
    full = (1, rows, width)
    sent_shape = (3, rows, half)
    *outs, sent = call(
        lambda *refs: backward_kernel(scale, heads, *refs),
        place,
        (groups,),
        own_in
        + [packed_in, (align_ids, smem), (align_count, smem)]
        + [(cg_own, feature_block), (cg_peer, feature_block)],
        [(full, b16, half_of(lambda y: y, groups))] * 3
        + [(sent_shape, b16, pl.BlockSpec((3, rows, group), lambda j, p: (0, 0, j)))],
        (groups * heads * 2**26, 5 * MIB, groups * heads * 2**16),
    )
    near_2e = send_edge(near_2m, near_1x, diagonal, sent)
    grad_p = pick((grad_2e, grad_3e), (grad_2m, grad_3m))
    grad_px = send_x(grad_p)
    near_1y = send_y(near_1)
    near_3e = send_edge(near_3m, near_1y)
    near_p = pick((near_2e, near_3e), (near_2m, near_3m))
    near_px = send_x(near_p)
    near_py = send_y(near_p)
    received = send_y(sent)
    diagonal_1 = send_edge(diagonal, grad_px)
    diagonal_2m = send_middle(diagonal)
    diagonal_2e = flipped("dp", 2)(diagonal_2m, near_3e)
    diagonal_3m = send_middle(diagonal_1)
    grad_1c = send_core(grad_1)
    grad_pc = send_core(grad_p)
    grad_xc = send_core(grad_x)
    grad_1xc = send_core(grad_1x)
    grad_pxc = send_core(grad_px)

    outs = call(
        place_kernel,
        place,
        (1,),
        [(received, whole(sent_shape))] + [(out, hbm) for out in outs],
        [(full, b16, peer_half)] * 3,
        (0, 12 * rows * half, 0),
        {2 + i: i for i in range(3)},
    )

    shape = (width, columns)
    def parts(first, second, pair, first_x, second_x, pair_x):
        return [first, second, (pair, 0), (pair, 1), first_x, second_x, (pair_x, 0), (pair_x, 1)]

    straight = parts((out_grad, 0), grad_1, grad_p, grad_x, grad_1x, grad_px)
    crossed = parts((out_grad, 0), grad_1c, grad_pc, grad_xc, grad_1xc, grad_pxc)
    near = [(c, c) for c in parts(context, near_1, near_p, context_x, near_1x, near_px)]
    near_place = jnp.stack([y, t, 1 - t, is_middle])
    far_place = jnp.stack([1 - y, t, 1 - t, is_middle])
    early = len(near) - 2
    part = weight_rows(
        near_place, near[:early], straight[:early], crossed[:early], None, None, None
    )
    diagonal_3e = send_edge(diagonal_3m, part)
    far = [(c, c) for c in (context_y, near_1y, (near_py, 0), (near_py, 1), diagonal, diagonal_1)]
    far += [(diagonal_2e, diagonal_2m), (diagonal_3e, diagonal_3m)]
    grad = weight_rows(
        near_place, near[early:], straight[early:], crossed[early:], part, None, shape
    )
    grad = weight_rows(far_place, far, straight, crossed, None, grad, shape)
    return (*outs, grad)


def shards(queries, key_states, value_states, out_grad, out_weight, align_ids, align_count):
    two_spans = lax.axis_size("span") == 2 and queries.shape[1] == SPAN == key_states.shape[1]
    if two_spans and lax.axis_size("dp") == 8 and lax.axis_size("tensor") == 2:
        return paired(
            queries, key_states, value_states, out_grad, out_weight, align_ids, align_count
        )
    f32 = jnp.float32
    b16 = jnp.bfloat16
    scale = 1.0 / math.sqrt(HEAD_DIM)
    local_width = queries.shape[2]
    local_heads = local_width // HEAD_DIM
    target_rows = queries.shape[1]
    source_rows = key_states.shape[1]
    span_number = target_rows // SPAN
    block_number = source_rows // BLOCK
    grad_rows = out_grad[0]
    context_grad = (
        lax.psum_scatter(
            lax.dot_general(
                grad_rows, out_weight, (((1,), (1,)), ((), ())), preferred_element_type=f32
            ).astype(jnp.bfloat16),
            "span",
            scatter_dimension=0,
            tiled=True,
        )
        .astype(jnp.float32)
        .astype(b16)
    )
    stacked = jnp.stack([key_states[0], value_states[0]])
    panel = with_halo(stacked, (("span", 1),), source_rows)
    position = lax.axis_index("span")
    local_ids = align_ids[0] - (position - 1) * block_number
    panel_blocks = panel.reshape(2, 3 * block_number, BLOCK, local_width)
    fetched = panel_blocks[:, local_ids]
    key_near = fetched[0].reshape(span_number, ALIGN * BLOCK, local_heads, HEAD_DIM)
    value_near = fetched[1].reshape(span_number, ALIGN * BLOCK, local_heads, HEAD_DIM)
    query_heads = queries[0].reshape(span_number, SPAN, local_heads, HEAD_DIM)
    live = (jnp.arange(ALIGN * BLOCK) // BLOCK)[None, :] < align_count[0][:, None]
    mask = live[:, None, None, :]
    scores = (
        jnp.einsum("nqhd,nkhd->nhqk", query_heads, key_near, preferred_element_type=f32) * scale
    )
    masked = jnp.where(mask, scores, -1e30)
    top = jnp.max(masked, axis=-1, keepdims=True)
    weights = jnp.where(mask, jnp.exp(masked - top), 0.0)
    prob = weights / jnp.sum(weights, axis=-1, keepdims=True)
    prob_half = prob.astype(b16)
    context = jnp.einsum(
        "nhqk,nkhd->nqhd", prob_half, value_near, preferred_element_type=f32
    ).astype(b16)
    grad_heads = context_grad.reshape(span_number, SPAN, local_heads, HEAD_DIM)
    dprob = jnp.einsum("nqhd,nkhd->nhqk", grad_heads, value_near, preferred_element_type=f32)
    delta = jnp.einsum("nqhd,nqhd->nhq", grad_heads, context, preferred_element_type=f32)[..., None]
    dscore = (prob * (dprob - delta)).astype(b16)
    query_grad = (
        jnp.einsum("nhqk,nkhd->nqhd", dscore, key_near, preferred_element_type=f32) * scale
    ).astype(b16)
    key_term = (
        jnp.einsum("nhqk,nqhd->nkhd", dscore, query_heads, preferred_element_type=f32) * scale
    )
    value_term = jnp.einsum("nhqk,nqhd->nkhd", prob_half, grad_heads, preferred_element_type=f32)
    slot_terms = jnp.stack([key_term, value_term]).reshape(
        2, span_number * ALIGN, BLOCK, local_width
    )
    flat_ids = local_ids.reshape(span_number * ALIGN)
    spread = (
        jnp.zeros((2, 3 * block_number, BLOCK, local_width), f32).at[:, flat_ids].add(slot_terms)
    )
    spread = spread.reshape(2, 3 * source_rows, local_width)
    lower_rim = spread[:, :source_rows].astype(b16)
    upper_rim = spread[:, 2 * source_rows :].astype(b16)
    from_above = shifted(lower_rim, "span", -1)
    from_below = shifted(upper_rim, "span", 1)
    summed = (
        spread[:, source_rows : 2 * source_rows] + from_above.astype(f32) + from_below.astype(f32)
    )
    pair_grad = summed.astype(b16)
    flat_context = context.reshape(target_rows, local_width)
    documents = lax.axis_size("dp")
    tokens = documents * grad_rows.shape[0]
    columns = grad_rows.shape[1]
    if tokens * (local_width + columns) <= 2 * local_width * columns:
        cores = lax.axis_size("tensor")
        share = grad_rows.shape[0] // cores
        own_share = lax.dynamic_slice_in_dim(
            grad_rows, lax.axis_index("tensor") * share, share, axis=0
        )
        all_grad = lax.all_gather(own_share, ("dp", "tensor"), axis=0, tiled=True)
        all_context = lax.all_gather(flat_context, ("dp", "span"), axis=0, tiled=True)
        weight_grad = lax.dot_general(
            all_context, all_grad, (((0,), (0,)), ((), ())), preferred_element_type=f32
        )
    else:
        gathered = lax.all_gather(flat_context, "span", axis=0, tiled=True)
        partial_grad = lax.dot_general(
            gathered, grad_rows, (((0,), (0,)), ((), ())), preferred_element_type=f32
        )
        weight_grad = lax.psum(partial_grad, "dp")
    query_out = query_grad.reshape(1, target_rows, local_width)
    return (query_out, pair_grad[0][None], pair_grad[1][None], weight_grad)


def solution(mesh):
    return jax.shard_map(
        shards,
        mesh=mesh,
        in_specs=(
            P("dp", "span", "tensor"),
            P("dp", "span", "tensor"),
            P("dp", "span", "tensor"),
            P("dp", None, "span"),
            P("tensor", "span"),
            P("dp", "span", None),
            P("dp", "span"),
        ),
        out_specs=(
            P("dp", "span", "tensor"),
            P("dp", "span", "tensor"),
            P("dp", "span", "tensor"),
            P("tensor", "span"),
        ),
        check_vma=False,
    )
```
